128 devices in a mesh: dp: 8 (over x, y_hi), tensor: 16 (over z, y_lo, core).
Axes of the slice: x: 4, y: 4 (y_hi: 2, y_lo: 2; y = y_hi * 2 + y_lo), z: 4, core: 2. Of those that a mesh axis runs over, the one named last changes fastest.
Arguments:
- grad_out: bfloat16 [2048, 9216], P(('dp', 'tensor')), may hold values from -0.3984375 to 0.3984375
- pre: bfloat16 [2048, 36864], P('dp', 'tensor'), may hold values from -6 to 6
- codes: int32 [36864, 9216], P('tensor', 'dp'), may hold values from 0 to 15
- exponents: int32 [288, 9216], P('tensor', 'dp'), may hold values from -7 to -4
Outputs:
- grad_pre: bfloat16 [2048, 36864], P('dp', 'tensor')
- grad_weight: float32 [36864, 9216], P('tensor', 'dp')
- grad_exponent: float32 [288, 9216], P('tensor', 'dp')
The draws below stay inside these ranges and needn't reach their ends.
All inputs are finite; a program needn't handle non-finite values.
Results may differ from the reference program's by a relative error of at most 0.0028.
Values may be sent and summed in bfloat16 or wider, within the bound.
A program may use at most 128 MiB of HBM per device.

```python
import jax
import jax.numpy as jnp
from jax import lax

D = 9216
FF = 36864
GROUP = 128
TOKENS = 2048


def plant(drawn, key, low, high):
    dims = drawn.shape
    place = [jax.random.randint(jax.random.fold_in(key, axis), (), 0, dims[axis]) for axis in range(len(dims))]
    drawn = drawn.at[tuple(place)].set(low)
    longest = dims.index(max(dims))
    place[longest] = (place[longest] + 1) % dims[longest]
    return drawn.at[tuple(place)].set(high)


def level_of(rng, shape, pieces, smallest, top_value):
    def one(dim, parts):
        heights = jax.random.uniform(jax.random.fold_in(jax.random.fold_in(rng, 6), dim), (parts,), jnp.float32, smallest / len(pieces), top_value / len(pieces))
        return jnp.repeat(jnp.exp(heights), shape[dim] // parts).reshape((-1,) + (1,) * (len(shape) - dim - 1))

    loudness = one(*pieces[0])
    for cut in pieces[1:]:
        loudness = loudness * one(*cut)
    return loudness


def scatter_about(stream_key, shape, width, bound, pieces=(), held_as=jnp.bfloat16):
    level = level_of(stream_key, shape, pieces, -0.22, 0.18) if pieces else 1.0
    values = jax.random.normal(stream_key, shape, jnp.float32) * width * level
    return jnp.minimum(jnp.maximum(values, -bound), bound).astype(held_as)


def setup_inputs(seed: int = 0) -> dict:
    key_of = jax.random.split(jax.random.key(seed), 5)
    return {
        "grad_out": scatter_about(key_of[0], (TOKENS, D), 0.05, 0.3984375, ((0, 128),)),
        "pre": scatter_about(key_of[1], (TOKENS, FF), 1.0, 6.0, ((0, 8), (1, 16))),
        "codes": plant(jax.random.randint(key_of[2], (FF, D), 0, 16), jax.random.fold_in(key_of[2], 1), 0, 15).astype(jnp.int32),
        "exponents": plant(jax.random.randint(key_of[3], (FF // GROUP, D), -7, -3), jax.random.fold_in(key_of[3], 1), -7, (-3) - 1).astype(jnp.int32),
    }


LOG_TWO = 0.6931471805599453


def scale_of(exponents):
    scale = jnp.zeros(exponents.shape, jnp.float32)
    for power in range(-7, -3):
        scale = scale + jnp.where(exponents == power, 2.0 ** power, 0.0).astype(jnp.float32)
    return scale


def reference(grad_out, pre, codes, exponents):
    groups = FF // GROUP
    code_blocks = codes.reshape(groups, GROUP, D)
    scales = scale_of(exponents)
    pre_blocks = pre.reshape(TOKENS, groups, GROUP).transpose(1, 0, 2)

    def one_group(items):
        code, scale, block = items
        weight = ((code - 8).astype(jnp.float32) * scale[None, :]).astype(jnp.bfloat16)
        positive = jnp.maximum(block.astype(jnp.float32), 0.0)
        act = (positive * positive).astype(jnp.bfloat16)
        grad_act = jnp.dot(grad_out, weight.T, preferred_element_type=jnp.float32)
        grad_block = (grad_act * 2.0 * positive).astype(jnp.bfloat16)
        grad_w = jnp.dot(act.T, grad_out, preferred_element_type=jnp.float32)
        grad_e = LOG_TWO * jnp.sum(grad_w * weight.astype(jnp.float32), axis=0)
        return grad_block, grad_w, grad_e

    grad_blocks, grad_ws, grad_es = lax.map(one_group, (code_blocks, scales, pre_blocks))
    grad_pre = grad_blocks.transpose(1, 0, 2).reshape(TOKENS, FF)
    grad_weight = grad_ws.reshape(FF, D)
    return grad_pre, grad_weight, grad_es
```

```python
import functools

import jax
import jax.numpy as jnp
from jax import lax
from jax.experimental import pallas as pl
from jax.experimental.pallas import tpu as pltpu
from jax.sharding import PartitionSpec as P

MESH = pl.DeviceIdType.MESH
LOG_TWO = 0.6931471805599453
NT = (((1,), (1,)), ((), ()))
BF16, F32, I16 = jnp.bfloat16, jnp.float32, jnp.int16

FF = 2304
WIDTH = 1152
ROWS = 256
HALF = ROWS // 2
GROUP = 128
LANES = 128
FX = 1280
FY = FF - FX
AX = 1024
AY = FF - AX
TOP = 32700.0
UNIT = TOP * TOP
CHUNK = 256
N_GW = FF // CHUNK
SLOTS = 3


def encode(value):
    root = value * lax.rsqrt(jnp.maximum(jnp.abs(value), 1e-20))
    return jnp.round(root).astype(I16)


def decode(code):
    root = code.astype(jnp.int32).astype(F32)
    return root * jnp.abs(root)


def add_into(target, others, step=16):
    def some(i, carry):
        rows = pl.ds(pl.multiple_of(i * step, step), step)
        total = decode(target[rows, :])
        for other in others:
            total = total + decode(other[rows, :])
        target[rows, :] = encode(total)
        return carry

    lax.fori_loop(0, target.shape[0] // step, some, 0)


def kernel(
    go_ref, pre_ref, codes_ref, exp_ref, gp_ref, gw_ref, ge_ref,
    act, pq, g, w, gsrc, cbuf, gwbuf,
    x1a, x1b, xm, xp, xc, y1, ya, yb, ym, yp,
    ssem, rsem, csem, gwsem,
):
    j = lax.axis_index("dp")
    t = lax.axis_index("tensor")
    x, yh = j // 2, j % 2
    other = 1 - yh
    z, yl, core = t // 4, (t // 2) % 2, t % 2

    def blk(dx, hi):
        return ((x + dx) % 4) * 2 + hi

    def ten(dz):
        return ((z + dz) % 4) * 4 + yl * 2 + core

    east, west = (blk(1, yh), t), (blk(3, yh), t)
    across = (blk(0, other), t)
    up, down = (j, ten(1)), (j, ten(3))
    beside = (j, z * 4 + (1 - yl) * 2 + core)
    twin = (j, z * 4 + yl * 2 + 1 - core)
    peers = [((j + k) % 8, t) for k in range(1, 8)]

    barrier = pltpu.get_barrier_semaphore()
    for device in (*peers, up, down, beside, twin):
        pl.semaphore_signal(barrier, inc=1, device_id=device, device_id_type=MESH)

    copies = {}

    def send(name, src, dst, device):
        n = len(copies)
        copy = pltpu.make_async_remote_copy(
            src_ref=src, dst_ref=dst, send_sem=ssem.at[n], recv_sem=rsem.at[n],
            device_id=device, device_id_type=MESH,
        )
        copy.start()
        copies[name] = copy

    def same(name, view, device):
        send(name, view, view, device)

    def arrive(*names):
        for name in names:
            copies[name].wait_recv()

    def fetch(i):
        slot = lax.rem(i, SLOTS)
        rows = pl.ds(pl.multiple_of(i * CHUNK, CHUNK), CHUNK)
        return pltpu.make_async_copy(codes_ref.at[rows, :], cbuf.at[slot], csem.at[slot])

    for i in range(SLOTS):
        fetch(i).start()

    total = jnp.zeros((16, 1), F32)
    for d in range(8):
        block = go_ref[:, d * WIDTH : (d + 1) * WIDTH]
        total = total + jnp.sum(jnp.abs(block.astype(F32)), axis=1, keepdims=True)
        gsrc[d, :, :WIDTH] = block
    scale = jnp.maximum(total * 0.51, 1e-36).astype(BF16)
    for d in range(8):
        gsrc[d, :, WIDTH:] = jnp.broadcast_to(scale, (16, LANES))
    mine = pl.ds(pl.multiple_of(t * 16, 16), 16)
    g[j, mine, :] = gsrc[j]

    def transpose(i, carry):
        columns = pl.ds(pl.multiple_of(i * LANES, LANES), LANES)
        positive = jnp.maximum(pre_ref[:, columns].astype(F32), 0.0)
        act[j, columns, :] = (positive * positive).astype(BF16).T
        return carry

    lax.fori_loop(0, FF // LANES, transpose, 0)

    pl.semaphore_wait(barrier, 11)

    for k in range(1, 8):
        d = (j + k) % 8
        send(f"a2a{k}", gsrc.at[d], g.at[j, mine, :], (d, t))

    def x_rows(b, part=None):
        if part is None:
            return act.at[b, pl.ds(0, AX), :]
        return act.at[b, pl.ds(part * (AX // 2), AX // 2), :]

    def y_rows(b, part=None):
        if part is None:
            return act.at[b, pl.ds(AX, AY), :]
        return act.at[b, pl.ds(AX + part * (AY // 2), AY // 2), :]

    same("ax+", x_rows(j), east)
    same("ax-", x_rows(j), west)
    same("ay", y_rows(j), across)

    def dequantize(i, carry):
        fetch(i).wait()
        slot = lax.rem(i, SLOTS)
        for half in range(CHUNK // GROUP):
            exponent = exp_ref[pl.ds(i * (CHUNK // GROUP) + half, 1), :]
            power = jnp.zeros(exponent.shape, F32)
            for p in range(-7, -3):
                power = jnp.where(exponent == p, 2.0**p, power)
            code = cbuf[slot, half * GROUP : (half + 1) * GROUP, :]
            rows = pl.ds(pl.multiple_of(i * CHUNK + half * GROUP, GROUP), GROUP)
            w[rows, :] = ((code - 8).astype(F32) * power).astype(BF16)

        @pl.when(i + SLOTS < N_GW)
        def _():
            fetch(i + SLOTS).start()

        return carry

    lax.fori_loop(0, N_GW, dequantize, 0)

    def tokens(dz, hi, part=None):
        rows = pl.ds(pl.multiple_of((((z + dz) % 4) * 4 + hi * 2 + core) * 16, 16), 16)
        if part is None:
            return g.at[:, rows, :]
        return g.at[pl.ds(part * 4, 4), rows, :]

    arrive(*(f"a2a{k}" for k in range(1, 8)))
    same("gl", tokens(0, yl), beside)
    same("g+", tokens(0, yl), up)
    same("g-", tokens(0, yl), down)
    same("gc0", tokens(0, yl), twin)

    same("ay+", y_rows(j), east)
    same("ay-", y_rows(j), west)
    same("axy", x_rows(j), across)

    arrive("gl")
    same("gl+", tokens(0, 1 - yl), up)
    same("gl-", tokens(0, 1 - yl), down)
    same("gc1", tokens(0, 1 - yl), twin)

    def products(dz):
        zz = (z + dz) % 4
        rows = pl.ds(pl.multiple_of(zz * 64, 64), 64)
        size = 768

        def some(n, carry):
            columns = pl.ds(pl.multiple_of(n * size, size), size)
            part = lax.dot_general(
                g[:, rows, pl.ds(0, WIDTH)].reshape(512, WIDTH), w[columns, :], NT, preferred_element_type=F32
            )
            inverse = UNIT / g[:, rows, pl.ds(WIDTH, LANES)].astype(F32).reshape(512, LANES)
            part = part * jnp.concatenate([inverse] * (size // LANES), axis=1)
            pq[:, rows, columns] = encode(part).reshape(8, 64, size)
            return carry

        lax.fori_loop(0, FF // size, some, 0)

    arrive("gc0", "gc1")
    products(0)

    arrive("g+")
    same("gf+", tokens(3, yl, 0), up)
    same("gc2", tokens(3, yl), twin)
    arrive("g-")
    same("gf-", tokens(1, yl, 1), down)
    same("gc3", tokens(1, yl), twin)

    arrive("ax+")
    same("axf+", x_rows(blk(3, yh), 0), east)
    same("axy1", x_rows(blk(3, yh)), across)
    arrive("ax-")
    same("axf-", x_rows(blk(1, yh), 1), west)
    same("axy2", x_rows(blk(1, yh)), across)
    arrive("ay")
    same("ayp+", y_rows(blk(0, other)), east)
    same("ayp-", y_rows(blk(0, other)), west)

    arrive("gl+")
    same("glf+", tokens(3, 1 - yl, 0), up)
    same("gc4", tokens(3, 1 - yl), twin)
    arrive("gl-")
    same("glf-", tokens(1, 1 - yl, 1), down)
    same("gc5", tokens(1, 1 - yl), twin)

    arrive("gc2", "gc4")
    products(3)
    arrive("ay+")
    same("ayf+", y_rows(blk(3, yh), 0), east)
    arrive("ay-")
    same("ayf-", y_rows(blk(1, yh), 1), west)

    arrive("gf+", "gf-", "glf+", "glf-")
    same("gc6", tokens(2, yl), twin)
    same("gc7", tokens(2, 1 - yl), twin)
    arrive("gc3", "gc5")
    products(1)
    arrive("axf+")
    same("axy3", x_rows(blk(2, yh), 0), across)
    arrive("axf-")
    same("axy4", x_rows(blk(2, yh), 1), across)

    arrive("gc6", "gc7")
    products(2)

    low, high, whole = pl.ds(0, HALF), pl.ds(HALF, HALF), pl.ds(0, ROWS)
    cx, cy = pl.ds(0, FX), pl.ds(FX, FY)

    for e in (1, 0):
        hi = other if e else yh
        send(f"h1+{e}", pq.at[blk(2, hi), low, cx], x1a.at[e], east)
        send(f"h1-{e}", pq.at[blk(2, hi), high, cx], x1b.at[e], west)
        if e:
            send("s2", pq.at[blk(2, other), whole, cy], y1.at[2], across)
            send("s1", pq.at[blk(1, other), whole, cy], y1.at[1], across)
            send("s3", pq.at[blk(3, other), whole, cy], y1.at[3], across)
    for e in (1, 0):
        hi = other if e else yh
        send(f"h2+{e}", pq.at[blk(1, hi), high, cx], xm.at[e, high, :], east)
        send(f"h2-{e}", pq.at[blk(3, hi), low, cx], xp.at[e, low, :], west)
    send("s0", pq.at[blk(0, other), whole, cy], y1.at[0], across)

    arrive("ayp+")
    same("aypf+", y_rows(blk(3, other), 0), east)
    arrive("ayp-")
    same("aypf-", y_rows(blk(1, other), 1), west)

    def relay(e):
        hi = other if e else yh
        arrive(f"h1+{e}")
        add_into(pq.at[blk(1, hi), low, cx], [x1a.at[e]])
        send(f"h3+{e}", pq.at[blk(1, hi), low, cx], xm.at[e, low, :], east)
        arrive(f"h1-{e}")
        add_into(pq.at[blk(3, hi), high, cx], [x1b.at[e]])
        send(f"h3-{e}", pq.at[blk(3, hi), high, cx], xp.at[e, high, :], west)

    relay(1)
    arrive("s2")
    add_into(pq.at[blk(2, yh), whole, cy], [y1.at[2]])
    send("t1+", pq.at[blk(2, yh), low, cy], ya, east)
    send("t1-", pq.at[blk(2, yh), high, cy], yb, west)
    relay(0)

    def store(i, slot):
        rows = pl.ds(pl.multiple_of(i * CHUNK, CHUNK), CHUNK)
        return pltpu.make_async_copy(gwbuf.at[slot], gw_ref.at[rows, :], gwsem.at[slot])

    def weight_tiles(first):
        def some(slot, carry):
            i = first + slot
            if first:
                store(i - SLOTS, slot).wait()
            rows = pl.ds(pl.multiple_of(i * CHUNK, CHUNK), CHUNK)
            left = jnp.concatenate([act[b, rows, :] for b in range(8)], axis=1)
            right = g[:, :, pl.ds(0, WIDTH)].reshape(8 * ROWS, WIDTH)
            tile = jnp.dot(left, right, preferred_element_type=F32)
            gwbuf[slot] = tile
            store(i, slot).start()
            product = tile * w[rows, :].astype(F32)
            ge_ref[i] = LOG_TWO * jnp.sum(product.reshape(CHUNK // GROUP, GROUP, WIDTH), axis=1)
            return carry

        lax.fori_loop(0, SLOTS, some, 0)

    arrive("axy", "axy1", "axy2", "axy3", "axy4", "ayf+", "ayf-", "aypf+", "aypf-")
    weight_tiles(0)

    arrive("s1")
    add_into(pq.at[blk(1, yh), high, cy], [y1.at[1, high, :]])
    send("t2+", pq.at[blk(1, yh), high, cy], ym.at[high, :], east)
    arrive("s3")
    add_into(pq.at[blk(3, yh), low, cy], [y1.at[3, low, :]])
    send("t2-", pq.at[blk(3, yh), low, cy], yp.at[low, :], west)
    arrive("t1+")
    add_into(pq.at[blk(1, yh), low, cy], [y1.at[1, low, :], ya])
    send("t3+", pq.at[blk(1, yh), low, cy], ym.at[low, :], east)
    arrive("t1-")
    add_into(pq.at[blk(3, yh), high, cy], [y1.at[3, high, :], yb])
    send("t3-", pq.at[blk(3, yh), high, cy], yp.at[high, :], west)

    weight_tiles(SLOTS)

    arrive("h2+1", "h2-1", "h3+1", "h3-1")
    add_into(pq.at[blk(0, other), whole, cx], [xm.at[1], xp.at[1]])
    send("c", pq.at[blk(0, other), whole, cx], xc, across)

    weight_tiles(2 * SLOTS)

    def finish(columns, parts):
        step = 16

        def some(i, carry):
            rows = pl.ds(pl.multiple_of(i * step, step), step)
            total = decode(pq[j, rows, columns])
            for part in parts:
                total = total + decode(part[rows, :])
            unit = g[j, rows, pl.ds(WIDTH, LANES)].astype(F32) * (2.0 / UNIT)
            positive = jnp.maximum(pre_ref[rows, columns].astype(F32), 0.0)
            unit = jnp.concatenate([unit] * (columns.size // LANES), axis=1)
            gp_ref[rows, columns] = (total * unit * positive).astype(BF16)
            return carry

        lax.fori_loop(0, ROWS // step, some, 0)

    arrive("s0", "t2+", "t2-", "t3+", "t3-")
    finish(cy, [y1.at[0], ym, yp])
    arrive("h2+0", "h2-0", "h3+0", "h3-0", "c")
    finish(cx, [xm.at[0], xp.at[0], xc])

    for slot in range(SLOTS):
        store(2 * SLOTS + slot, slot).wait()
    for copy in copies.values():
        copy.wait_send()


def body(grad_out, pre, codes, exponents):
    vmem, hbm = pl.BlockSpec(memory_space=pltpu.VMEM), pl.BlockSpec(memory_space=pl.ANY)
    n_copies = 72
    grad_pre, grad_weight, grad_exponent = pl.pallas_call(
        kernel,
        out_shape=(
            jax.ShapeDtypeStruct((ROWS, FF), BF16),
            jax.ShapeDtypeStruct((FF, WIDTH), F32),
            jax.ShapeDtypeStruct((N_GW, CHUNK // GROUP, WIDTH), F32),
        ),
        in_specs=[vmem, vmem, hbm, vmem],
        out_specs=(vmem, hbm, vmem),
        scratch_shapes=[
            pltpu.VMEM((8, FF, ROWS), BF16),
            pltpu.VMEM((8, ROWS, FF), I16),
            pltpu.VMEM((8, ROWS, WIDTH + LANES), BF16),
            pltpu.VMEM((FF, WIDTH), BF16),
            pltpu.VMEM((8, 16, WIDTH + LANES), BF16),
            pltpu.VMEM((SLOTS, CHUNK, WIDTH), jnp.int32),
            pltpu.VMEM((SLOTS, CHUNK, WIDTH), F32),
            pltpu.VMEM((2, HALF, FX), I16),
            pltpu.VMEM((2, HALF, FX), I16),
            pltpu.VMEM((2, ROWS, FX), I16),
            pltpu.VMEM((2, ROWS, FX), I16),
            pltpu.VMEM((ROWS, FX), I16),
            pltpu.VMEM((4, ROWS, FY), I16),
            pltpu.VMEM((HALF, FY), I16),
            pltpu.VMEM((HALF, FY), I16),
            pltpu.VMEM((ROWS, FY), I16),
            pltpu.VMEM((ROWS, FY), I16),
            pltpu.SemaphoreType.DMA((n_copies,)),
            pltpu.SemaphoreType.DMA((n_copies,)),
            pltpu.SemaphoreType.DMA((SLOTS,)),
            pltpu.SemaphoreType.DMA((SLOTS,)),
        ],
        compiler_params=pltpu.CompilerParams(
            collective_id=0, has_side_effects=True, vmem_limit_bytes=60 * 2**20
        ),
        name="backward",
    )(grad_out, pre, codes, exponents)
    return grad_pre, grad_weight, grad_exponent.reshape(exponents.shape)


def solution(mesh):
    return jax.shard_map(
        body,
        mesh=mesh,
        in_specs=(
            P(("dp", "tensor"), None),
            P("dp", "tensor"),
            P("tensor", "dp"),
            P("tensor", "dp"),
        ),
        out_specs=(P("dp", "tensor"), P("tensor", "dp"), P("tensor", "dp")),
        check_vma=False,
    )
```

```python
import functools

import jax
import jax.numpy as jnp
from jax import lax
from jax.experimental import pallas as pl
from jax.experimental.pallas import tpu as pltpu
from jax.sharding import PartitionSpec as P

MESH = pl.DeviceIdType.MESH
LOG_TWO = 0.6931471805599453
NT = (((1,), (1,)), ((), ()))
BF16, F32, I16 = jnp.bfloat16, jnp.float32, jnp.int16

FF = 2304
WIDTH = 1152
ROWS = 256
HALF = ROWS // 2
GROUP = 128
LANES = 128
FX = 1280
FY = FF - FX
AX = 896
AY1 = 768
AY2 = FF - AX - AY1
TOP = 32700.0
UNIT = TOP * TOP
CHUNK = 256
N_GW = FF // CHUNK
SLOTS = 3


def encode(value):
    root = value * lax.rsqrt(jnp.maximum(jnp.abs(value), 1e-20))
    return jnp.round(root).astype(I16)


def decode(code):
    root = code.astype(jnp.int32).astype(F32)
    return root * jnp.abs(root)


def add_into(target, others, step=16):
    def some(i, carry):
        rows = pl.ds(pl.multiple_of(i * step, step), step)
        total = decode(target[rows, :])
        for other in others:
            total = total + decode(other[rows, :])
        target[rows, :] = encode(total)
        return carry

    lax.fori_loop(0, target.shape[0] // step, some, 0)


def kernel(
    go_hbm, pre_hbm, codes_ref, exp_hbm, gp_ref, gw_ref, ge_ref,
    go_ref, pre_ref, exp_ref, act, pq, g, w, gsrc, cbuf,
    x1a, x1b, xm, xp, xc, y1, ya, yb, ym, yp,
    ssem, rsem, csem, isem,
):
    j = lax.axis_index("dp")
    t = lax.axis_index("tensor")
    x, yh = j // 2, j % 2
    other = 1 - yh
    z, yl, core = t // 4, (t // 2) % 2, t % 2

    def blk(dx, hi):
        return ((x + dx) % 4) * 2 + hi

    def ten(dz):
        return ((z + dz) % 4) * 4 + yl * 2 + core

    east, west = (blk(1, yh), t), (blk(3, yh), t)
    across = (blk(0, other), t)
    up, down = (j, ten(1)), (j, ten(3))
    beside = (j, z * 4 + (1 - yl) * 2 + core)
    twin = (j, z * 4 + yl * 2 + 1 - core)
    peers = [((j + k) % 8, t) for k in range(1, 8)]

    barrier = pltpu.get_barrier_semaphore()
    for device in (*peers, up, down, beside, twin):
        pl.semaphore_signal(barrier, inc=1, device_id=device, device_id_type=MESH)

    copies = {}

    def send(name, src, dst, device):
        n = len(copies)
        copy = pltpu.make_async_remote_copy(
            src_ref=src, dst_ref=dst, send_sem=ssem.at[n], recv_sem=rsem.at[n],
            device_id=device, device_id_type=MESH,
        )
        copy.start()
        copies[name] = copy

    def same(name, view, device):
        send(name, view, view, device)

    def arrive(*names):
        for name in names:
            copies[name].wait_recv()

    def fetch(i):
        slot = lax.rem(i, SLOTS)
        rows = pl.ds(pl.multiple_of(i * CHUNK, CHUNK), CHUNK)
        return pltpu.make_async_copy(codes_ref.at[rows, :], cbuf.at[slot], csem.at[slot])

    for i in range(SLOTS):
        fetch(i).start()

    spans = [pl.ds(AX, AY1), pl.ds(0, AX), pl.ds(AX + AY1, AY2)]
    loads = [pltpu.make_async_copy(go_hbm, go_ref, isem.at[0])]
    for n, span in enumerate(spans):
        loads.append(pltpu.make_async_copy(pre_hbm.at[:, span], pre_ref.at[:, span], isem.at[1 + n]))
    loads.append(pltpu.make_async_copy(exp_hbm, exp_ref, isem.at[4]))
    for load in loads:
        load.start()

    loads[0].wait()
    total = jnp.zeros((16, 1), F32)
    for d in range(8):
        block = go_ref[:, d * WIDTH : (d + 1) * WIDTH]
        total = total + jnp.sum(jnp.abs(block.astype(F32)), axis=1, keepdims=True)
        gsrc[d, :, :WIDTH] = block
    scale = jnp.maximum(total * 0.51, 1e-36).astype(BF16)
    for d in range(8):
        gsrc[d, :, WIDTH:] = jnp.broadcast_to(scale, (16, LANES))
    mine = pl.ds(pl.multiple_of(t * 16, 16), 16)
    g[j, mine, :] = gsrc[j]

    pl.semaphore_wait(barrier, 11)

    for k in range(1, 8):
        d = (j + k) % 8
        send(f"a2a{k}", gsrc.at[d], g.at[j, mine, :], (d, t))

    def transpose(i, carry):
        columns = pl.ds(pl.multiple_of(i * LANES, LANES), LANES)
        positive = jnp.maximum(pre_ref[:, columns].astype(F32), 0.0)
        act[j, columns, :] = (positive * positive).astype(BF16).T
        return carry

    def piece(first, size):
        def rows(b, part=None):
            if part is None:
                return act.at[b, pl.ds(first, size), :]
            return act.at[b, pl.ds(first + part * (size // 2), size // 2), :]

        return rows

    y1_rows, x_rows, y2_rows = piece(AX, AY1), piece(0, AX), piece(AX + AY1, AY2)

    loads[1].wait()
    lax.fori_loop(AX // LANES, (AX + AY1) // LANES, transpose, 0)
    same("ay1", y1_rows(j), across)
    same("ay1+", y1_rows(j), east)
    same("ay1-", y1_rows(j), west)
    loads[2].wait()
    lax.fori_loop(0, AX // LANES, transpose, 0)
    same("ax+", x_rows(j), east)
    same("ax-", x_rows(j), west)
    loads[3].wait()
    lax.fori_loop((AX + AY1) // LANES, FF // LANES, transpose, 0)
    loads[4].wait()

    def dequantize(i, carry):
        fetch(i).wait()
        slot = lax.rem(i, SLOTS)
        for half in range(CHUNK // GROUP):
            exponent = exp_ref[pl.ds(i * (CHUNK // GROUP) + half, 1), :]
            power = jnp.zeros(exponent.shape, F32)
            for p in range(-7, -3):
                power = jnp.where(exponent == p, 2.0**p, power)
            code = cbuf[slot, half * GROUP : (half + 1) * GROUP, :]
            rows = pl.ds(pl.multiple_of(i * CHUNK + half * GROUP, GROUP), GROUP)
            w[rows, :] = ((code - 8).astype(F32) * power).astype(BF16)

        @pl.when(i + SLOTS < N_GW)
        def _():
            fetch(i + SLOTS).start()

        return carry

    lax.fori_loop(0, N_GW, dequantize, 0)

    def tokens(dz, hi, part=None):
        rows = pl.ds(pl.multiple_of((((z + dz) % 4) * 4 + hi * 2 + core) * 16, 16), 16)
        if part is None:
            return g.at[:, rows, :]
        return g.at[pl.ds(part * 4, 4), rows, :]

    arrive(*(f"a2a{k}" for k in range(1, 8)))
    same("gl", tokens(0, yl), beside)
    same("g+", tokens(0, yl), up)
    same("g-", tokens(0, yl), down)
    same("gc0", tokens(0, yl), twin)
    same("ay2", y2_rows(j), across)
    same("axy", x_rows(j), across)

    arrive("ay1")
    same("ayp1+", y1_rows(blk(0, other)), east)
    same("ayp1-", y1_rows(blk(0, other)), west)
    same("ay2+", y2_rows(j), east)
    same("ay2-", y2_rows(j), west)
    arrive("g+")
    same("gf+", tokens(3, yl, 0), up)
    same("gc2", tokens(3, yl), twin)
    arrive("g-")
    same("gf-", tokens(1, yl, 1), down)
    same("gc3", tokens(1, yl), twin)
    arrive("ay1+")
    same("ayf1+", y1_rows(blk(3, yh), 0), east)
    arrive("ay1-")
    same("ayf1-", y1_rows(blk(1, yh), 1), west)

    arrive("gl")
    same("gl+", tokens(0, 1 - yl), up)
    same("gl-", tokens(0, 1 - yl), down)
    same("gc1", tokens(0, 1 - yl), twin)

    def products(dz):
        zz = (z + dz) % 4
        rows = pl.ds(pl.multiple_of(zz * 64, 64), 64)
        size = 768

        def some(n, carry):
            columns = pl.ds(pl.multiple_of(n * size, size), size)
            part = lax.dot_general(
                g[:, rows, pl.ds(0, WIDTH)].reshape(512, WIDTH), w[columns, :], NT, preferred_element_type=F32
            )
            inverse = UNIT / g[:, rows, pl.ds(WIDTH, LANES)].astype(F32).reshape(512, LANES)
            part = part * jnp.concatenate([inverse] * (size // LANES), axis=1)
            pq[:, rows, columns] = encode(part).reshape(8, 64, size)
            return carry

        lax.fori_loop(0, FF // size, some, 0)

    arrive("gc0", "gc1")
    products(0)

    arrive("ax+")
    same("axf+", x_rows(blk(3, yh), 0), east)
    same("axy1", x_rows(blk(3, yh)), across)
    arrive("ax-")
    same("axf-", x_rows(blk(1, yh), 1), west)
    same("axy2", x_rows(blk(1, yh)), across)

    arrive("gl+")
    same("glf+", tokens(3, 1 - yl, 0), up)
    same("gc4", tokens(3, 1 - yl), twin)
    arrive("gl-")
    same("glf-", tokens(1, 1 - yl, 1), down)
    same("gc5", tokens(1, 1 - yl), twin)
    arrive("ay2")
    same("ayp2+", y2_rows(blk(0, other)), east)
    same("ayp2-", y2_rows(blk(0, other)), west)

    arrive("gc2", "gc4")
    products(3)
    arrive("gf+", "gf-", "glf+", "glf-")
    same("gc6", tokens(2, yl), twin)
    same("gc7", tokens(2, 1 - yl), twin)
    arrive("ay2+")
    same("ayf2+", y2_rows(blk(3, yh), 0), east)
    arrive("ay2-")
    same("ayf2-", y2_rows(blk(1, yh), 1), west)
    arrive("ayp1+")
    same("aypf1+", y1_rows(blk(3, other), 0), east)
    arrive("ayp1-")
    same("aypf1-", y1_rows(blk(1, other), 1), west)
    arrive("gc3", "gc5")
    products(1)
    arrive("gc6", "gc7")
    products(2)
    arrive("axf+")
    same("axy3", x_rows(blk(2, yh), 0), across)
    arrive("axf-")
    same("axy4", x_rows(blk(2, yh), 1), across)

    low, high, whole = pl.ds(0, HALF), pl.ds(HALF, HALF), pl.ds(0, ROWS)
    cx, cy = pl.ds(0, FX), pl.ds(FX, FY)

    def first(e):
        hi = other if e else yh
        send(f"h1+{e}", pq.at[blk(2, hi), low, cx], x1a.at[e], east)
        send(f"h1-{e}", pq.at[blk(2, hi), high, cx], x1b.at[e], west)

    def second(e):
        hi = other if e else yh
        send(f"h2+{e}", pq.at[blk(1, hi), high, cx], xm.at[e, high, :], east)
        send(f"h2-{e}", pq.at[blk(3, hi), low, cx], xp.at[e, low, :], west)

    first(1)
    for k in (2, 1, 3, 0):
        send(f"s{k}", pq.at[blk(k, other), whole, cy], y1.at[k], across)
    arrive("ayp2+")
    same("aypf2+", y2_rows(blk(3, other), 0), east)
    arrive("ayp2-")
    same("aypf2-", y2_rows(blk(1, other), 1), west)
    first(0)
    second(1)
    second(0)

    def relay(e):
        hi = other if e else yh
        arrive(f"h1+{e}")
        add_into(pq.at[blk(1, hi), low, cx], [x1a.at[e]])
        send(f"h3+{e}", pq.at[blk(1, hi), low, cx], xm.at[e, low, :], east)
        arrive(f"h1-{e}")
        add_into(pq.at[blk(3, hi), high, cx], [x1b.at[e]])
        send(f"h3-{e}", pq.at[blk(3, hi), high, cx], xp.at[e, high, :], west)

    relay(1)
    arrive("s2")
    add_into(pq.at[blk(2, yh), whole, cy], [y1.at[2]])
    send("t1+", pq.at[blk(2, yh), low, cy], ya, east)
    send("t1-", pq.at[blk(2, yh), high, cy], yb, west)
    relay(0)

    def weight_tiles(first):
        def some(slot, carry):
            i = first + slot
            rows = pl.ds(pl.multiple_of(i * CHUNK, CHUNK), CHUNK)
            left = jnp.concatenate([act[b, rows, :] for b in range(8)], axis=1)
            right = g[:, :, pl.ds(0, WIDTH)].reshape(8 * ROWS, WIDTH)
            tile = jnp.dot(left, right, preferred_element_type=F32)
            gw_ref[rows, :] = tile
            product = tile * w[rows, :].astype(F32)
            ge_ref[i] = LOG_TWO * jnp.sum(product.reshape(CHUNK // GROUP, GROUP, WIDTH), axis=1)
            return carry

        lax.fori_loop(0, SLOTS, some, 0)

    arrive("axy", "axy1", "axy2", "axy3", "axy4")
    arrive(*(f"{name}{n}{way}" for name in ("ayf", "aypf") for n in "12" for way in "+-"))
    weight_tiles(0)

    arrive("s1")
    add_into(pq.at[blk(1, yh), high, cy], [y1.at[1, high, :]])
    send("t2+", pq.at[blk(1, yh), high, cy], ym.at[high, :], east)
    arrive("s3")
    add_into(pq.at[blk(3, yh), low, cy], [y1.at[3, low, :]])
    send("t2-", pq.at[blk(3, yh), low, cy], yp.at[low, :], west)
    arrive("t1+")
    add_into(pq.at[blk(1, yh), low, cy], [y1.at[1, low, :], ya])
    send("t3+", pq.at[blk(1, yh), low, cy], ym.at[low, :], east)
    arrive("t1-")
    add_into(pq.at[blk(3, yh), high, cy], [y1.at[3, high, :], yb])
    send("t3-", pq.at[blk(3, yh), high, cy], yp.at[high, :], west)

    weight_tiles(SLOTS)

    arrive("h2+1", "h2-1", "h3+1", "h3-1")
    halves = [pl.ds(0, FX // 2), pl.ds(FX // 2, FX // 2)]
    for n, part in enumerate(halves):
        add_into(pq.at[blk(0, other), whole, part], [xm.at[1, :, part], xp.at[1, :, part]])
        send(f"c{n}", pq.at[blk(0, other), whole, part], xc.at[:, part], across)

    weight_tiles(2 * SLOTS)

    def finish(columns, parts):
        step = 16

        def some(i, carry):
            rows = pl.ds(pl.multiple_of(i * step, step), step)
            total = decode(pq[j, rows, columns])
            for part in parts:
                total = total + decode(part[rows, :])
            unit = g[j, rows, pl.ds(WIDTH, LANES)].astype(F32) * (2.0 / UNIT)
            positive = jnp.maximum(pre_ref[rows, columns].astype(F32), 0.0)
            unit = jnp.concatenate([unit] * (columns.size // LANES), axis=1)
            gp_ref[rows, columns] = (total * unit * positive).astype(BF16)
            return carry

        lax.fori_loop(0, ROWS // step, some, 0)

    arrive("h2+0", "h2-0", "h3+0", "h3-0", "c0")
    finish(halves[0], [r.at[:, halves[0]] for r in (xm.at[0], xp.at[0], xc)])
    arrive("s0", "t2+", "t2-", "t3+", "t3-")
    finish(cy, [y1.at[0], ym, yp])
    arrive("c1")
    finish(halves[1], [r.at[:, halves[1]] for r in (xm.at[0], xp.at[0], xc)])

    for copy in copies.values():
        copy.wait_send()


def place(gp, gw, ge, gp_out, gw_out, ge_out, rows, sem):
    copies = []
    for i in range(N_GW):
        part = pl.ds(i * CHUNK, CHUNK)
        copies.append(pltpu.make_async_copy(gw.at[part, :], gw_out.at[part, :], sem.at[i]))
    copies.append(pltpu.make_async_copy(gp, gp_out, sem.at[N_GW]))
    for copy in copies:
        copy.start()
    per = CHUNK // GROUP
    for i in range(N_GW):
        rows[i * per : (i + 1) * per, :] = ge[i]
    last = pltpu.make_async_copy(rows, ge_out, sem.at[N_GW + 1])
    last.start()
    for copy in (*copies, last):
        copy.wait()


def body(grad_out, pre, codes, exponents):
    vmem, hbm = pl.BlockSpec(memory_space=pltpu.VMEM), pl.BlockSpec(memory_space=pl.ANY)
    n_copies = 80
    grad_pre, grad_weight, grad_exponent = pl.pallas_call(
        kernel,
        out_shape=(
            pltpu.VMEM((ROWS, FF), BF16),
            pltpu.VMEM((FF, WIDTH), F32),
            pltpu.VMEM((N_GW, CHUNK // GROUP, WIDTH), F32),
        ),
        in_specs=[pl.BlockSpec(memory_space=pltpu.HBM)] * 4,
        out_specs=(vmem, vmem, vmem),
        scratch_shapes=[
            pltpu.VMEM((16, 8 * WIDTH), BF16),
            pltpu.VMEM((ROWS, FF), BF16),
            pltpu.VMEM(exponents.shape, jnp.int32),
            pltpu.VMEM((8, FF, ROWS), BF16),
            pltpu.VMEM((8, ROWS, FF), I16),
            pltpu.VMEM((8, ROWS, WIDTH + LANES), BF16),
            pltpu.VMEM((FF, WIDTH), BF16),
            pltpu.VMEM((8, 16, WIDTH + LANES), BF16),
            pltpu.VMEM((SLOTS, CHUNK, WIDTH), jnp.int32),
            pltpu.VMEM((2, HALF, FX), I16),
            pltpu.VMEM((2, HALF, FX), I16),
            pltpu.VMEM((2, ROWS, FX), I16),
            pltpu.VMEM((2, ROWS, FX), I16),
            pltpu.VMEM((ROWS, FX), I16),
            pltpu.VMEM((4, ROWS, FY), I16),
            pltpu.VMEM((HALF, FY), I16),
            pltpu.VMEM((HALF, FY), I16),
            pltpu.VMEM((ROWS, FY), I16),
            pltpu.VMEM((ROWS, FY), I16),
            pltpu.SemaphoreType.DMA((n_copies,)),
            pltpu.SemaphoreType.DMA((n_copies,)),
            pltpu.SemaphoreType.DMA((SLOTS,)),
            pltpu.SemaphoreType.DMA((5,)),
        ],
        compiler_params=pltpu.CompilerParams(
            collective_id=0, has_side_effects=True, vmem_limit_bytes=46 * 2**20
        ),
        name="backward",
    )(grad_out, pre, codes, exponents)
    return pl.pallas_call(
        place,
        out_shape=(
            jax.ShapeDtypeStruct((ROWS, FF), BF16),
            jax.ShapeDtypeStruct((FF, WIDTH), F32),
            jax.ShapeDtypeStruct(exponents.shape, F32),
        ),
        in_specs=[vmem] * 3,
        out_specs=(hbm, hbm, hbm),
        scratch_shapes=[
            pltpu.VMEM(exponents.shape, F32),
            pltpu.SemaphoreType.DMA((N_GW + 2,)),
        ],
        compiler_params=pltpu.CompilerParams(vmem_limit_bytes=4 * 2**20),
        name="place",
    )(grad_pre, grad_weight, grad_exponent)


def solution(mesh):
    return jax.shard_map(
        body,
        mesh=mesh,
        in_specs=(
            P(("dp", "tensor"), None),
            P("dp", "tensor"),
            P("tensor", "dp"),
            P("tensor", "dp"),
        ),
        out_specs=(P("dp", "tensor"), P("tensor", "dp"), P("tensor", "dp")),
        check_vma=False,
    )
```

```python
import functools

import jax
import jax.numpy as jnp
from jax import lax
from jax.experimental import pallas as pl
from jax.experimental.pallas import tpu as pltpu
from jax.sharding import PartitionSpec as P

MESH = pl.DeviceIdType.MESH
LOG_TWO = 0.6931471805599453
NT = (((1,), (1,)), ((), ()))
BF16, F32, I16 = jnp.bfloat16, jnp.float32, jnp.int16

FF = 2304
WIDTH = 1152
ROWS = 256
HALF = ROWS // 2
GROUP = 128
LANES = 128
FX = 1280
FY = FF - FX
PIECES = (512, 384, 256, 128)
AX = 896
AY1 = 768
AY2 = FF - AX - AY1
TOP = 32700.0
UNIT = TOP * TOP
CHUNK = 256
N_GW = FF // CHUNK
SLOTS = 3


def encode(value):
    root = value * lax.rsqrt(jnp.maximum(jnp.abs(value), 1e-20))
    return jnp.round(root).astype(I16)


def decode(code):
    root = code.astype(jnp.int32).astype(F32)
    return root * jnp.abs(root)


def add_into(target, others, step=16):
    def some(i, carry):
        rows = pl.ds(pl.multiple_of(i * step, step), step)
        total = decode(target[rows, :])
        for other in others:
            total = total + decode(other[rows, :])
        target[rows, :] = encode(total)
        return carry

    lax.fori_loop(0, target.shape[0] // step, some, 0)


def kernel(
    go_hbm, pre_hbm, codes_ref, exp_hbm, gp_ref, gw_ref, ge_ref,
    go_ref, pre_ref, exp_ref, act, pq, g, w, gsrc, cbuf,
    x1a, x1b, xm, xp, xc, y1, ya, yb, ym, yp,
    ssem, rsem, csem, isem,
):
    j = lax.axis_index("dp")
    t = lax.axis_index("tensor")
    x, yh = j // 2, j % 2
    other = 1 - yh
    z, yl, core = t // 4, (t // 2) % 2, t % 2

    def blk(dx, hi):
        return ((x + dx) % 4) * 2 + hi

    def ten(dz):
        return ((z + dz) % 4) * 4 + yl * 2 + core

    east, west = (blk(1, yh), t), (blk(3, yh), t)
    across = (blk(0, other), t)
    up, down = (j, ten(1)), (j, ten(3))
    beside = (j, z * 4 + (1 - yl) * 2 + core)
    twin = (j, z * 4 + yl * 2 + 1 - core)
    peers = [((j + k) % 8, t) for k in range(1, 8)]

    barrier = pltpu.get_barrier_semaphore()
    for device in (*peers, up, down, beside, twin):
        pl.semaphore_signal(barrier, inc=1, device_id=device, device_id_type=MESH)

    copies = {}

    def send(name, src, dst, device):
        n = len(copies)
        copy = pltpu.make_async_remote_copy(
            src_ref=src, dst_ref=dst, send_sem=ssem.at[n], recv_sem=rsem.at[n],
            device_id=device, device_id_type=MESH,
        )
        copy.start()
        copies[name] = copy

    def same(name, view, device):
        send(name, view, view, device)

    def arrive(*names):
        for name in names:
            copies[name].wait_recv()

    spans = [pl.ds(AX, AY1), pl.ds(0, AX), pl.ds(AX + AY1, AY2)]
    pieces = []
    for n, span in enumerate(spans):
        pieces.append(pltpu.make_async_copy(pre_hbm.at[:, span], pre_ref.at[:, span], isem.at[n]))
    rows_load = pltpu.make_async_copy(go_hbm, go_ref, isem.at[3])
    exponents_load = pltpu.make_async_copy(exp_hbm, exp_ref, isem.at[4])
    for load in (pieces[0], rows_load, pieces[1], pieces[2], exponents_load):
        load.start()

    def fetch(i):
        slot = lax.rem(i, SLOTS)
        rows = pl.ds(pl.multiple_of(i * CHUNK, CHUNK), CHUNK)
        return pltpu.make_async_copy(codes_ref.at[rows, :], cbuf.at[slot], csem.at[slot])

    for i in range(SLOTS):
        fetch(i).start()

    def transpose(i, carry):
        columns = pl.ds(pl.multiple_of(i * LANES, LANES), LANES)
        positive = jnp.maximum(pre_ref[:, columns].astype(F32), 0.0)
        act[j, columns, :] = (positive * positive).astype(BF16).T
        return carry

    def piece(first, size):
        def rows(b, part=None):
            if part is None:
                return act.at[b, pl.ds(first, size), :]
            return act.at[b, pl.ds(first + part * (size // 2), size // 2), :]

        return rows

    y1_rows, x_rows, y2_rows = piece(AX, AY1), piece(0, AX), piece(AX + AY1, AY2)

    pieces[0].wait()
    lax.fori_loop(AX // LANES, (AX + AY1) // LANES, transpose, 0)

    rows_load.wait()
    total = jnp.zeros((16, 1), F32)
    for d in range(8):
        block = go_ref[:, d * WIDTH : (d + 1) * WIDTH]
        total = total + jnp.sum(jnp.abs(block.astype(F32)), axis=1, keepdims=True)
        gsrc[d, :, :WIDTH] = block
    scale = jnp.maximum(total * 0.51, 1e-36).astype(BF16)
    for d in range(8):
        gsrc[d, :, WIDTH:] = jnp.broadcast_to(scale, (16, LANES))
    mine = pl.ds(pl.multiple_of(t * 16, 16), 16)
    g[j, mine, :] = gsrc[j]

    pl.semaphore_wait(barrier, 11)

    for k in range(1, 8):
        d = (j + k) % 8
        send(f"a2a{k}", gsrc.at[d], g.at[j, mine, :], (d, t))
    same("ay1", y1_rows(j), across)
    same("ay1+", y1_rows(j), east)
    same("ay1-", y1_rows(j), west)
    pieces[1].wait()
    lax.fori_loop(0, AX // LANES, transpose, 0)
    same("ax+", x_rows(j), east)
    same("ax-", x_rows(j), west)
    pieces[2].wait()
    lax.fori_loop((AX + AY1) // LANES, FF // LANES, transpose, 0)
    exponents_load.wait()

    def dequantize(i, carry):
        fetch(i).wait()
        slot = lax.rem(i, SLOTS)
        for half in range(CHUNK // GROUP):
            exponent = exp_ref[pl.ds(i * (CHUNK // GROUP) + half, 1), :]
            power = jnp.zeros(exponent.shape, F32)
            for p in range(-7, -3):
                power = jnp.where(exponent == p, 2.0**p, power)
            code = cbuf[slot, half * GROUP : (half + 1) * GROUP, :]
            rows = pl.ds(pl.multiple_of(i * CHUNK + half * GROUP, GROUP), GROUP)
            w[rows, :] = ((code - 8).astype(F32) * power).astype(BF16)

        @pl.when(i + SLOTS < N_GW)
        def _():
            fetch(i + SLOTS).start()

        return carry

    lax.fori_loop(0, N_GW, dequantize, 0)

    def tokens(dz, hi, part=None):
        rows = pl.ds(pl.multiple_of((((z + dz) % 4) * 4 + hi * 2 + core) * 16, 16), 16)
        if part is None:
            return g.at[:, rows, :]
        return g.at[pl.ds(part * 4, 4), rows, :]

    arrive(*(f"a2a{k}" for k in range(1, 8)))
    same("gl", tokens(0, yl), beside)
    same("g+", tokens(0, yl), up)
    same("g-", tokens(0, yl), down)
    same("gc0", tokens(0, yl), twin)
    same("ay2", y2_rows(j), across)
    same("axy", x_rows(j), across)

    arrive("ay1")
    same("ayp1+", y1_rows(blk(0, other)), east)
    same("ayp1-", y1_rows(blk(0, other)), west)
    same("ay2+", y2_rows(j), east)
    same("ay2-", y2_rows(j), west)
    arrive("g+")
    same("gf+", tokens(3, yl, 0), up)
    same("gc2", tokens(3, yl), twin)
    arrive("g-")
    same("gf-", tokens(1, yl, 1), down)
    same("gc3", tokens(1, yl), twin)
    arrive("ay1+")
    same("ayf1+", y1_rows(blk(3, yh), 0), east)
    arrive("ay1-")
    same("ayf1-", y1_rows(blk(1, yh), 1), west)

    arrive("gl")
    same("gl+", tokens(0, 1 - yl), up)
    same("gl-", tokens(0, 1 - yl), down)
    same("gc1", tokens(0, 1 - yl), twin)

    def products(dz):
        zz = (z + dz) % 4
        rows = pl.ds(pl.multiple_of(zz * 64, 64), 64)
        size = 768

        def some(n, carry):
            columns = pl.ds(pl.multiple_of(n * size, size), size)
            part = lax.dot_general(
                g[:, rows, pl.ds(0, WIDTH)].reshape(512, WIDTH), w[columns, :], NT, preferred_element_type=F32
            )
            inverse = UNIT / g[:, rows, pl.ds(WIDTH, LANES)].astype(F32).reshape(512, LANES)
            part = part * jnp.concatenate([inverse] * (size // LANES), axis=1)
            pq[:, rows, columns] = encode(part).reshape(8, 64, size)
            return carry

        lax.fori_loop(0, FF // size, some, 0)

    arrive("gc0", "gc1")
    products(0)

    arrive("ax+")
    same("axf+", x_rows(blk(3, yh), 0), east)
    same("axy1", x_rows(blk(3, yh)), across)
    arrive("ax-")
    same("axf-", x_rows(blk(1, yh), 1), west)
    same("axy2", x_rows(blk(1, yh)), across)

    arrive("gl+")
    same("glf+", tokens(3, 1 - yl, 0), up)
    same("gc4", tokens(3, 1 - yl), twin)
    arrive("gl-")
    same("glf-", tokens(1, 1 - yl, 1), down)
    same("gc5", tokens(1, 1 - yl), twin)
    arrive("ay2")
    same("ayp2+", y2_rows(blk(0, other)), east)
    same("ayp2-", y2_rows(blk(0, other)), west)

    arrive("gc2", "gc4")
    products(3)
    arrive("gf+", "gf-", "glf+", "glf-")
    same("gc6", tokens(2, yl), twin)
    same("gc7", tokens(2, 1 - yl), twin)
    arrive("ay2+")
    same("ayf2+", y2_rows(blk(3, yh), 0), east)
    arrive("ay2-")
    same("ayf2-", y2_rows(blk(1, yh), 1), west)
    arrive("ayp1+")
    same("aypf1+", y1_rows(blk(3, other), 0), east)
    arrive("ayp1-")
    same("aypf1-", y1_rows(blk(1, other), 1), west)
    arrive("gc3", "gc5")
    products(1)
    arrive("gc6", "gc7")
    products(2)
    arrive("axf+")
    same("axy3", x_rows(blk(2, yh), 0), across)
    arrive("axf-")
    same("axy4", x_rows(blk(2, yh), 1), across)

    low, high, whole = pl.ds(0, HALF), pl.ds(HALF, HALF), pl.ds(0, ROWS)
    cx, cy = pl.ds(0, FX), pl.ds(FX, FY)

    def first(e):
        hi = other if e else yh
        send(f"h1+{e}", pq.at[blk(2, hi), low, cx], x1a.at[e], east)
        send(f"h1-{e}", pq.at[blk(2, hi), high, cx], x1b.at[e], west)

    def second(e):
        hi = other if e else yh
        send(f"h2+{e}", pq.at[blk(1, hi), high, cx], xm.at[e, high, :], east)
        send(f"h2-{e}", pq.at[blk(3, hi), low, cx], xp.at[e, low, :], west)

    first(1)
    for k in (2, 1, 3, 0):
        send(f"s{k}", pq.at[blk(k, other), whole, cy], y1.at[k], across)
    arrive("ayp2+")
    same("aypf2+", y2_rows(blk(3, other), 0), east)
    arrive("ayp2-")
    same("aypf2-", y2_rows(blk(1, other), 1), west)
    first(0)
    second(1)

    def relay(e):
        hi = other if e else yh
        arrive(f"h1+{e}")
        add_into(pq.at[blk(1, hi), low, cx], [x1a.at[e]])
        send(f"h3+{e}", pq.at[blk(1, hi), low, cx], xm.at[e, low, :], east)
        arrive(f"h1-{e}")
        add_into(pq.at[blk(3, hi), high, cx], [x1b.at[e]])
        send(f"h3-{e}", pq.at[blk(3, hi), high, cx], xp.at[e, high, :], west)

    relay(1)
    arrive("s2")
    add_into(pq.at[blk(2, yh), whole, cy], [y1.at[2]])
    send("t1+", pq.at[blk(2, yh), low, cy], ya, east)
    send("t1-", pq.at[blk(2, yh), high, cy], yb, west)
    second(0)
    relay(0)

    def weight_tiles(first):
        def some(slot, carry):
            i = first + slot
            rows = pl.ds(pl.multiple_of(i * CHUNK, CHUNK), CHUNK)
            left = jnp.concatenate([act[b, rows, :] for b in range(8)], axis=1)
            right = g[:, :, pl.ds(0, WIDTH)].reshape(8 * ROWS, WIDTH)
            tile = jnp.dot(left, right, preferred_element_type=F32)
            gw_ref[rows, :] = tile
            product = tile * w[rows, :].astype(F32)
            ge_ref[i] = LOG_TWO * jnp.sum(product.reshape(CHUNK // GROUP, GROUP, WIDTH), axis=1)
            return carry

        lax.fori_loop(0, SLOTS, some, 0)

    arrive("axy", "axy1", "axy2", "axy3", "axy4")
    arrive(*(f"{name}{n}{way}" for name in ("ayf", "aypf") for n in "12" for way in "+-"))
    weight_tiles(0)
    weight_tiles(SLOTS)

    arrive("s1")
    add_into(pq.at[blk(1, yh), high, cy], [y1.at[1, high, :]])
    send("t2+", pq.at[blk(1, yh), high, cy], ym.at[high, :], east)

    arrive("h2+1", "h2-1", "h3+1", "h3-1")
    spans, first_column = [], 0
    for size in PIECES:
        spans.append(pl.ds(first_column, size))
        first_column += size
    for n, part in enumerate(spans):
        add_into(pq.at[blk(0, other), whole, part], [xm.at[1, :, part], xp.at[1, :, part]])
        send(f"c{n}", pq.at[blk(0, other), whole, part], xc.at[:, part], across)

    arrive("s3")
    add_into(pq.at[blk(3, yh), low, cy], [y1.at[3, low, :]])
    send("t2-", pq.at[blk(3, yh), low, cy], yp.at[low, :], west)
    arrive("t1+")
    add_into(pq.at[blk(1, yh), low, cy], [y1.at[1, low, :], ya])
    send("t3+", pq.at[blk(1, yh), low, cy], ym.at[low, :], east)
    arrive("t1-")
    add_into(pq.at[blk(3, yh), high, cy], [y1.at[3, high, :], yb])
    send("t3-", pq.at[blk(3, yh), high, cy], yp.at[high, :], west)

    weight_tiles(2 * SLOTS)

    def finish(columns, parts):
        step = 16

        def some(i, carry):
            rows = pl.ds(pl.multiple_of(i * step, step), step)
            total = decode(pq[j, rows, columns])
            for part in parts:
                total = total + decode(part[rows, :])
            unit = g[j, rows, pl.ds(WIDTH, LANES)].astype(F32) * (2.0 / UNIT)
            positive = jnp.maximum(pre_ref[rows, columns].astype(F32), 0.0)
            unit = jnp.concatenate([unit] * (columns.size // LANES), axis=1)
            gp_ref[rows, columns] = (total * unit * positive).astype(BF16)
            return carry

        lax.fori_loop(0, ROWS // step, some, 0)

    def finish_x(n):
        arrive(f"c{n}")
        finish(spans[n], [r.at[:, spans[n]] for r in (xm.at[0], xp.at[0], xc)])

    arrive("h2+0", "h2-0", "h3+0", "h3-0")
    for n in range(len(PIECES) - 2):
        finish_x(n)
    arrive("s0", "t2+", "t2-", "t3+", "t3-")
    finish(cy, [y1.at[0], ym, yp])
    for n in range(len(PIECES) - 2, len(PIECES)):
        finish_x(n)

    for copy in copies.values():
        copy.wait_send()


def place(gp, gw, ge, gp_out, gw_out, ge_out, rows, sem):
    copies = []
    for i in range(N_GW):
        part = pl.ds(i * CHUNK, CHUNK)
        copies.append(pltpu.make_async_copy(gw.at[part, :], gw_out.at[part, :], sem.at[i]))
    copies.append(pltpu.make_async_copy(gp, gp_out, sem.at[N_GW]))
    for copy in copies:
        copy.start()
    per = CHUNK // GROUP
    for i in range(N_GW):
        rows[i * per : (i + 1) * per, :] = ge[i]
    last = pltpu.make_async_copy(rows, ge_out, sem.at[N_GW + 1])
    last.start()
    for copy in (*copies, last):
        copy.wait()


def body(grad_out, pre, codes, exponents):
    vmem, hbm = pl.BlockSpec(memory_space=pltpu.VMEM), pl.BlockSpec(memory_space=pl.ANY)
    n_copies = 80
    grad_pre, grad_weight, grad_exponent = pl.pallas_call(
        kernel,
        out_shape=(
            pltpu.VMEM((ROWS, FF), BF16),
            pltpu.VMEM((FF, WIDTH), F32),
            pltpu.VMEM((N_GW, CHUNK // GROUP, WIDTH), F32),
        ),
        in_specs=[pl.BlockSpec(memory_space=pltpu.HBM)] * 4,
        out_specs=(vmem, vmem, vmem),
        scratch_shapes=[
            pltpu.VMEM((16, 8 * WIDTH), BF16),
            pltpu.VMEM((ROWS, FF), BF16),
            pltpu.VMEM(exponents.shape, jnp.int32),
            pltpu.VMEM((8, FF, ROWS), BF16),
            pltpu.VMEM((8, ROWS, FF), I16),
            pltpu.VMEM((8, ROWS, WIDTH + LANES), BF16),
            pltpu.VMEM((FF, WIDTH), BF16),
            pltpu.VMEM((8, 16, WIDTH + LANES), BF16),
            pltpu.VMEM((SLOTS, CHUNK, WIDTH), jnp.int32),
            pltpu.VMEM((2, HALF, FX), I16),
            pltpu.VMEM((2, HALF, FX), I16),
            pltpu.VMEM((2, ROWS, FX), I16),
            pltpu.VMEM((2, ROWS, FX), I16),
            pltpu.VMEM((ROWS, FX), I16),
            pltpu.VMEM((4, ROWS, FY), I16),
            pltpu.VMEM((HALF, FY), I16),
            pltpu.VMEM((HALF, FY), I16),
            pltpu.VMEM((ROWS, FY), I16),
            pltpu.VMEM((ROWS, FY), I16),
            pltpu.SemaphoreType.DMA((n_copies,)),
            pltpu.SemaphoreType.DMA((n_copies,)),
            pltpu.SemaphoreType.DMA((SLOTS,)),
            pltpu.SemaphoreType.DMA((5,)),
        ],
        compiler_params=pltpu.CompilerParams(
            collective_id=0, has_side_effects=True, vmem_limit_bytes=46 * 2**20
        ),
        name="backward",
    )(grad_out, pre, codes, exponents)
    return pl.pallas_call(
        place,
        out_shape=(
            jax.ShapeDtypeStruct((ROWS, FF), BF16),
            jax.ShapeDtypeStruct((FF, WIDTH), F32),
            jax.ShapeDtypeStruct(exponents.shape, F32),
        ),
        in_specs=[vmem] * 3,
        out_specs=(hbm, hbm, hbm),
        scratch_shapes=[
            pltpu.VMEM(exponents.shape, F32),
            pltpu.SemaphoreType.DMA((N_GW + 2,)),
        ],
        compiler_params=pltpu.CompilerParams(vmem_limit_bytes=4 * 2**20),
        name="place",
    )(grad_pre, grad_weight, grad_exponent)


def solution(mesh):
    return jax.shard_map(
        body,
        mesh=mesh,
        in_specs=(
            P(("dp", "tensor"), None),
            P("dp", "tensor"),
            P("tensor", "dp"),
            P("tensor", "dp"),
        ),
        out_specs=(P("dp", "tensor"), P("tensor", "dp"), P("tensor", "dp")),
        check_vma=False,
    )
```

```python
import functools

import jax
import jax.numpy as jnp
from jax import lax
from jax.experimental import pallas as pl
from jax.experimental.pallas import tpu as pltpu
from jax.sharding import PartitionSpec as P

MESH = pl.DeviceIdType.MESH
LOG_TWO = 0.6931471805599453
NT = (((1,), (1,)), ((), ()))
BF16, F32, I16 = jnp.bfloat16, jnp.float32, jnp.int16

FF = 2304
WIDTH = 1152
ROWS = 256
HALF = ROWS // 2
GROUP = 128
LANES = 128
FX = 1280
FY = FF - FX
PIECES = (512, 384, 256, 128)
AX = 896
AY1 = 768
EARLY = 256
AY2 = FF - AX - AY1
TOP = 32700.0
UNIT = TOP * TOP
CHUNK = 256
N_GW = FF // CHUNK
SLOTS = 3


def encode(value):
    root = value * lax.rsqrt(jnp.maximum(jnp.abs(value), 1e-20))
    return jnp.round(root).astype(I16)


def decode(code):
    root = code.astype(jnp.int32).astype(F32)
    return root * jnp.abs(root)


def step_of(rows, columns):
    step = 16
    while step * 2 <= rows and step * 2 * columns <= 16 * 2048:
        step *= 2
    return step


def add_into(target, others):
    step = step_of(*target.shape)

    def some(i, carry):
        rows = pl.ds(pl.multiple_of(i * step, step), step)
        total = decode(target[rows, :])
        for other in others:
            total = total + decode(other[rows, :])
        target[rows, :] = encode(total)
        return carry

    lax.fori_loop(0, target.shape[0] // step, some, 0)


def kernel(
    go_hbm, pre_hbm, codes_ref, exp_hbm, gp_ref, gw_ref, ge_ref,
    go_ref, pre_ref, exp_ref, act, pq, g, w, gsrc, cbuf,
    x1a, x1b, xm, xp, xc, y1, ya, yb, ym, yp,
    ssem, rsem, csem, isem,
):
    j = lax.axis_index("dp")
    t = lax.axis_index("tensor")
    x, yh = j // 2, j % 2
    other = 1 - yh
    z, yl, core = t // 4, (t // 2) % 2, t % 2

    def blk(dx, hi):
        return ((x + dx) % 4) * 2 + hi

    def ten(dz):
        return ((z + dz) % 4) * 4 + yl * 2 + core

    east, west = (blk(1, yh), t), (blk(3, yh), t)
    across = (blk(0, other), t)
    up, down = (j, ten(1)), (j, ten(3))
    beside = (j, z * 4 + (1 - yl) * 2 + core)
    twin = (j, z * 4 + yl * 2 + 1 - core)
    peers = [((j + k) % 8, t) for k in range(1, 8)]

    barrier = pltpu.get_barrier_semaphore()
    for device in (*peers, up, down, beside, twin):
        pl.semaphore_signal(barrier, inc=1, device_id=device, device_id_type=MESH)

    copies = {}

    def send(name, src, dst, device):
        n = len(copies)
        copy = pltpu.make_async_remote_copy(
            src_ref=src, dst_ref=dst, send_sem=ssem.at[n], recv_sem=rsem.at[n],
            device_id=device, device_id_type=MESH,
        )
        copy.start()
        copies[name] = copy

    def same(name, view, device):
        send(name, view, view, device)

    def arrive(*names):
        for name in names:
            copies[name].wait_recv()

    spans = [pl.ds(AX, EARLY), pl.ds(AX + EARLY, AY1 - EARLY), pl.ds(0, AX), pl.ds(AX + AY1, AY2)]
    pieces = []
    for n, span in enumerate(spans):
        pieces.append(pltpu.make_async_copy(pre_hbm.at[:, span], pre_ref.at[:, span], isem.at[n]))
    rows_load = pltpu.make_async_copy(go_hbm, go_ref, isem.at[5])
    exponents_load = pltpu.make_async_copy(exp_hbm, exp_ref, isem.at[4])
    for load in (pieces[0], rows_load, *pieces[1:], exponents_load):
        load.start()

    def fetch(i):
        slot = lax.rem(i, SLOTS)
        rows = pl.ds(pl.multiple_of(i * CHUNK, CHUNK), CHUNK)
        return pltpu.make_async_copy(codes_ref.at[rows, :], cbuf.at[slot], csem.at[slot])

    for i in range(SLOTS):
        fetch(i).start()

    def transpose(i, carry):
        columns = pl.ds(pl.multiple_of(i * LANES, LANES), LANES)
        positive = jnp.maximum(pre_ref[:, columns].astype(F32), 0.0)
        act[j, columns, :] = (positive * positive).astype(BF16).T
        return carry

    def piece(first, size):
        def rows(b, part=None):
            if part is None:
                return act.at[b, pl.ds(first, size), :]
            return act.at[b, pl.ds(first + part * (size // 2), size // 2), :]

        return rows

    y1_rows, x_rows, y2_rows = piece(AX, AY1), piece(0, AX), piece(AX + AY1, AY2)

    pieces[0].wait()
    lax.fori_loop(AX // LANES, (AX + EARLY) // LANES, transpose, 0)

    def early(name, start, end):
        view = act.at[j, pl.ds(AX + start, end - start), :]
        same(name, view, across)
        same(f"{name}+", view, east)
        same(f"{name}-", view, west)

    pl.semaphore_wait(barrier, 11)
    early("ay0", 0, EARLY)

    rows_load.wait()
    total = jnp.zeros((16, 1), F32)
    for d in range(8):
        block = go_ref[:, d * WIDTH : (d + 1) * WIDTH]
        total = total + jnp.sum(jnp.abs(block.astype(F32)), axis=1, keepdims=True)
        gsrc[d, :, :WIDTH] = block
    scale = jnp.maximum(total * 0.51, 1e-36).astype(BF16)
    for d in range(8):
        gsrc[d, :, WIDTH:] = jnp.broadcast_to(scale, (16, LANES))
    mine = pl.ds(pl.multiple_of(t * 16, 16), 16)
    g[j, mine, :] = gsrc[j]


    for k in range(1, 8):
        d = (j + k) % 8
        send(f"a2a{k}", gsrc.at[d], g.at[j, mine, :], (d, t))
    pieces[1].wait()
    lax.fori_loop((AX + EARLY) // LANES, (AX + AY1) // LANES, transpose, 0)
    early("ay1", EARLY, AY1)
    pieces[2].wait()
    lax.fori_loop(0, AX // LANES, transpose, 0)
    same("ax+", x_rows(j), east)
    same("ax-", x_rows(j), west)
    pieces[3].wait()
    lax.fori_loop((AX + AY1) // LANES, FF // LANES, transpose, 0)
    exponents_load.wait()

    def dequantize(i, carry):
        fetch(i).wait()
        slot = lax.rem(i, SLOTS)
        for half in range(CHUNK // GROUP):
            exponent = exp_ref[pl.ds(i * (CHUNK // GROUP) + half, 1), :]
            power = jnp.zeros(exponent.shape, F32)
            for p in range(-7, -3):
                power = jnp.where(exponent == p, 2.0**p, power)
            code = cbuf[slot, half * GROUP : (half + 1) * GROUP, :]
            rows = pl.ds(pl.multiple_of(i * CHUNK + half * GROUP, GROUP), GROUP)
            w[rows, :] = ((code - 8).astype(F32) * power).astype(BF16)

        @pl.when(i + SLOTS < N_GW)
        def _():
            fetch(i + SLOTS).start()

        return carry

    lax.fori_loop(0, N_GW, dequantize, 0)

    def tokens(dz, hi, part=None):
        rows = pl.ds(pl.multiple_of((((z + dz) % 4) * 4 + hi * 2 + core) * 16, 16), 16)
        if part is None:
            return g.at[:, rows, :]
        return g.at[pl.ds(part * 4, 4), rows, :]

    arrive(*(f"a2a{k}" for k in range(1, 8)))
    same("gl", tokens(0, yl), beside)
    same("g+", tokens(0, yl), up)
    same("g-", tokens(0, yl), down)
    same("gc0", tokens(0, yl), twin)
    same("ay2", y2_rows(j), across)
    same("axy", x_rows(j), across)

    arrive("ay0", "ay1")
    same("ayp1+", y1_rows(blk(0, other)), east)
    same("ayp1-", y1_rows(blk(0, other)), west)
    same("ay2+", y2_rows(j), east)
    same("ay2-", y2_rows(j), west)
    arrive("g+")
    same("gf+", tokens(3, yl, 0), up)
    same("gc2", tokens(3, yl), twin)
    arrive("g-")
    same("gf-", tokens(1, yl, 1), down)
    same("gc3", tokens(1, yl), twin)
    arrive("ay0+", "ay1+")
    same("ayf1+", y1_rows(blk(3, yh), 0), east)
    arrive("ay0-", "ay1-")
    same("ayf1-", y1_rows(blk(1, yh), 1), west)

    arrive("gl")
    same("gl+", tokens(0, 1 - yl), up)
    same("gl-", tokens(0, 1 - yl), down)
    same("gc1", tokens(0, 1 - yl), twin)

    def products(dz):
        zz = (z + dz) % 4
        rows = pl.ds(pl.multiple_of(zz * 64, 64), 64)
        size = 768

        def some(n, carry):
            columns = pl.ds(pl.multiple_of(n * size, size), size)
            part = lax.dot_general(
                g[:, rows, pl.ds(0, WIDTH)].reshape(512, WIDTH), w[columns, :], NT, preferred_element_type=F32
            )
            inverse = UNIT / g[:, rows, pl.ds(WIDTH, LANES)].astype(F32).reshape(512, LANES)
            part = part * jnp.concatenate([inverse] * (size // LANES), axis=1)
            pq[:, rows, columns] = encode(part).reshape(8, 64, size)
            return carry

        lax.fori_loop(0, FF // size, some, 0)

    arrive("gc0", "gc1")
    products(0)

    arrive("ax+")
    same("axf+", x_rows(blk(3, yh), 0), east)
    same("axy1", x_rows(blk(3, yh)), across)
    arrive("ax-")
    same("axf-", x_rows(blk(1, yh), 1), west)
    same("axy2", x_rows(blk(1, yh)), across)

    arrive("gl+")
    same("glf+", tokens(3, 1 - yl, 0), up)
    same("gc4", tokens(3, 1 - yl), twin)
    arrive("gl-")
    same("glf-", tokens(1, 1 - yl, 1), down)
    same("gc5", tokens(1, 1 - yl), twin)
    arrive("ay2")
    same("ayp2+", y2_rows(blk(0, other)), east)
    same("ayp2-", y2_rows(blk(0, other)), west)

    arrive("gc2", "gc4")
    products(3)
    arrive("gf+", "gf-", "glf+", "glf-")
    same("gc6", tokens(2, yl), twin)
    same("gc7", tokens(2, 1 - yl), twin)
    arrive("ay2+")
    same("ayf2+", y2_rows(blk(3, yh), 0), east)
    arrive("ay2-")
    same("ayf2-", y2_rows(blk(1, yh), 1), west)
    arrive("ayp1+")
    same("aypf1+", y1_rows(blk(3, other), 0), east)
    arrive("ayp1-")
    same("aypf1-", y1_rows(blk(1, other), 1), west)
    arrive("gc3", "gc5")
    products(1)
    arrive("gc6", "gc7")
    products(2)
    arrive("axf+")
    same("axy3", x_rows(blk(2, yh), 0), across)
    arrive("axf-")
    same("axy4", x_rows(blk(2, yh), 1), across)

    low, high, whole = pl.ds(0, HALF), pl.ds(HALF, HALF), pl.ds(0, ROWS)
    cx, cy = pl.ds(0, FX), pl.ds(FX, FY)

    def first(e):
        hi = other if e else yh
        send(f"h1+{e}", pq.at[blk(2, hi), low, cx], x1a.at[e], east)
        send(f"h1-{e}", pq.at[blk(2, hi), high, cx], x1b.at[e], west)

    def second(e):
        hi = other if e else yh
        send(f"h2+{e}", pq.at[blk(1, hi), high, cx], xm.at[e, high, :], east)
        send(f"h2-{e}", pq.at[blk(3, hi), low, cx], xp.at[e, low, :], west)

    first(1)
    for k in (2, 1, 3, 0):
        send(f"s{k}", pq.at[blk(k, other), whole, cy], y1.at[k], across)
    arrive("ayp2+")
    same("aypf2+", y2_rows(blk(3, other), 0), east)
    arrive("ayp2-")
    same("aypf2-", y2_rows(blk(1, other), 1), west)
    first(0)
    second(1)

    def relay(e):
        hi = other if e else yh
        arrive(f"h1+{e}")
        add_into(pq.at[blk(1, hi), low, cx], [x1a.at[e]])
        send(f"h3+{e}", pq.at[blk(1, hi), low, cx], xm.at[e, low, :], east)
        arrive(f"h1-{e}")
        add_into(pq.at[blk(3, hi), high, cx], [x1b.at[e]])
        send(f"h3-{e}", pq.at[blk(3, hi), high, cx], xp.at[e, high, :], west)

    relay(1)
    arrive("s2")
    add_into(pq.at[blk(2, yh), whole, cy], [y1.at[2]])
    send("t1+", pq.at[blk(2, yh), low, cy], ya, east)
    send("t1-", pq.at[blk(2, yh), high, cy], yb, west)
    second(0)
    relay(0)

    def weight_tiles(first):
        def some(slot, carry):
            i = first + slot
            rows = pl.ds(pl.multiple_of(i * CHUNK, CHUNK), CHUNK)
            left = jnp.concatenate([act[b, rows, :] for b in range(8)], axis=1)
            right = g[:, :, pl.ds(0, WIDTH)].reshape(8 * ROWS, WIDTH)
            tile = jnp.dot(left, right, preferred_element_type=F32)
            gw_ref[rows, :] = tile
            product = tile * w[rows, :].astype(F32)
            ge_ref[i] = LOG_TWO * jnp.sum(product.reshape(CHUNK // GROUP, GROUP, WIDTH), axis=1)
            return carry

        lax.fori_loop(0, SLOTS, some, 0)

    arrive("axy", "axy1", "axy2", "axy3", "axy4")
    arrive(*(f"{name}{n}{way}" for name in ("ayf", "aypf") for n in "12" for way in "+-"))
    weight_tiles(0)
    weight_tiles(SLOTS)

    arrive("s1")
    add_into(pq.at[blk(1, yh), high, cy], [y1.at[1, high, :]])
    send("t2+", pq.at[blk(1, yh), high, cy], ym.at[high, :], east)

    arrive("h2+1", "h2-1", "h3+1", "h3-1")
    spans, first_column = [], 0
    for size in PIECES:
        spans.append(pl.ds(first_column, size))
        first_column += size
    for n, part in enumerate(spans):
        add_into(pq.at[blk(0, other), whole, part], [xm.at[1, :, part], xp.at[1, :, part]])
        send(f"c{n}", pq.at[blk(0, other), whole, part], xc.at[:, part], across)

    arrive("s3")
    add_into(pq.at[blk(3, yh), low, cy], [y1.at[3, low, :]])
    send("t2-", pq.at[blk(3, yh), low, cy], yp.at[low, :], west)
    arrive("t1+")
    add_into(pq.at[blk(1, yh), low, cy], [y1.at[1, low, :], ya])
    send("t3+", pq.at[blk(1, yh), low, cy], ym.at[low, :], east)
    arrive("t1-")
    add_into(pq.at[blk(3, yh), high, cy], [y1.at[3, high, :], yb])
    send("t3-", pq.at[blk(3, yh), high, cy], yp.at[high, :], west)

    weight_tiles(2 * SLOTS)

    def finish(columns, parts):
        step = step_of(ROWS, columns.size)

        def some(i, carry):
            rows = pl.ds(pl.multiple_of(i * step, step), step)
            total = decode(pq[j, rows, columns])
            for part in parts:
                total = total + decode(part[rows, :])
            unit = g[j, rows, pl.ds(WIDTH, LANES)].astype(F32) * (2.0 / UNIT)
            positive = jnp.maximum(pre_ref[rows, columns].astype(F32), 0.0)
            unit = jnp.concatenate([unit] * (columns.size // LANES), axis=1)
            gp_ref[rows, columns] = (total * unit * positive).astype(BF16)
            return carry

        lax.fori_loop(0, ROWS // step, some, 0)

    def finish_x(n):
        arrive(f"c{n}")
        finish(spans[n], [r.at[:, spans[n]] for r in (xm.at[0], xp.at[0], xc)])

    late = {"s0", "t2+", "t2-", "t3+", "t3-", *(f"c{n}" for n in range(len(PIECES)))}
    for name in copies:
        if name not in late:
            copies[name].wait_send()
    arrive("h2+0", "h2-0", "h3+0", "h3-0")
    for n in range(len(PIECES) - 2):
        finish_x(n)
    arrive("s0", "t2+", "t2-", "t3+", "t3-")
    finish(cy, [y1.at[0], ym, yp])
    for n in range(len(PIECES) - 2, len(PIECES)):
        finish_x(n)

    for name in copies:
        if name in late:
            copies[name].wait_send()


def place(gp, gw, ge, gp_out, gw_out, ge_out, rows, sem):
    copies = []
    for i in range(N_GW):
        part = pl.ds(i * CHUNK, CHUNK)
        copies.append(pltpu.make_async_copy(gw.at[part, :], gw_out.at[part, :], sem.at[i]))
    copies.append(pltpu.make_async_copy(gp, gp_out, sem.at[N_GW]))
    for copy in copies:
        copy.start()
    per = CHUNK // GROUP
    for i in range(N_GW):
        rows[i * per : (i + 1) * per, :] = ge[i]
    last = pltpu.make_async_copy(rows, ge_out, sem.at[N_GW + 1])
    last.start()
    for copy in (*copies, last):
        copy.wait()


def body(grad_out, pre, codes, exponents):
    vmem, hbm = pl.BlockSpec(memory_space=pltpu.VMEM), pl.BlockSpec(memory_space=pl.ANY)
    n_copies = 80
    grad_pre, grad_weight, grad_exponent = pl.pallas_call(
        kernel,
        out_shape=(
            pltpu.VMEM((ROWS, FF), BF16),
            pltpu.VMEM((FF, WIDTH), F32),
            pltpu.VMEM((N_GW, CHUNK // GROUP, WIDTH), F32),
        ),
        in_specs=[pl.BlockSpec(memory_space=pltpu.HBM)] * 4,
        out_specs=(vmem, vmem, vmem),
        scratch_shapes=[
            pltpu.VMEM((16, 8 * WIDTH), BF16),
            pltpu.VMEM((ROWS, FF), BF16),
            pltpu.VMEM(exponents.shape, jnp.int32),
            pltpu.VMEM((8, FF, ROWS), BF16),
            pltpu.VMEM((8, ROWS, FF), I16),
            pltpu.VMEM((8, ROWS, WIDTH + LANES), BF16),
            pltpu.VMEM((FF, WIDTH), BF16),
            pltpu.VMEM((8, 16, WIDTH + LANES), BF16),
            pltpu.VMEM((SLOTS, CHUNK, WIDTH), jnp.int32),
            pltpu.VMEM((2, HALF, FX), I16),
            pltpu.VMEM((2, HALF, FX), I16),
            pltpu.VMEM((2, ROWS, FX), I16),
            pltpu.VMEM((2, ROWS, FX), I16),
            pltpu.VMEM((ROWS, FX), I16),
            pltpu.VMEM((4, ROWS, FY), I16),
            pltpu.VMEM((HALF, FY), I16),
            pltpu.VMEM((HALF, FY), I16),
            pltpu.VMEM((ROWS, FY), I16),
            pltpu.VMEM((ROWS, FY), I16),
            pltpu.SemaphoreType.DMA((n_copies,)),
            pltpu.SemaphoreType.DMA((n_copies,)),
            pltpu.SemaphoreType.DMA((SLOTS,)),
            pltpu.SemaphoreType.DMA((6,)),
        ],
        compiler_params=pltpu.CompilerParams(
            collective_id=0, has_side_effects=True, vmem_limit_bytes=46 * 2**20
        ),
        name="backward",
    )(grad_out, pre, codes, exponents)
    return pl.pallas_call(
        place,
        out_shape=(
            jax.ShapeDtypeStruct((ROWS, FF), BF16),
            jax.ShapeDtypeStruct((FF, WIDTH), F32),
            jax.ShapeDtypeStruct(exponents.shape, F32),
        ),
        in_specs=[vmem] * 3,
        out_specs=(hbm, hbm, hbm),
        scratch_shapes=[
            pltpu.VMEM(exponents.shape, F32),
            pltpu.SemaphoreType.DMA((N_GW + 2,)),
        ],
        compiler_params=pltpu.CompilerParams(vmem_limit_bytes=4 * 2**20),
        name="place",
    )(grad_pre, grad_weight, grad_exponent)


def solution(mesh):
    return jax.shard_map(
        body,
        mesh=mesh,
        in_specs=(
            P(("dp", "tensor"), None),
            P("dp", "tensor"),
            P("tensor", "dp"),
            P("tensor", "dp"),
        ),
        out_specs=(P("dp", "tensor"), P("tensor", "dp"), P("tensor", "dp")),
        check_vma=False,
    )
```

```python
import functools

import jax
import jax.numpy as jnp
from jax import lax
from jax.experimental import pallas as pl
from jax.experimental.pallas import tpu as pltpu
from jax.sharding import PartitionSpec as P

MESH = pl.DeviceIdType.MESH
LOG_TWO = 0.6931471805599453
NT = (((1,), (1,)), ((), ()))
BF16, F32, I16 = jnp.bfloat16, jnp.float32, jnp.int16

FF = 2304
WIDTH = 1152
ROWS = 256
HALF = ROWS // 2
GROUP = 128
LANES = 128
FX = 1280
FY = FF - FX
PIECES = (112, 80, 48, 16)
AX = 896
AY1 = 768
EARLY = 256
AY2 = FF - AX - AY1
TOP = 32700.0
UNIT = TOP * TOP
CHUNK = 256
N_GW = FF // CHUNK
SLOTS = 3


def encode(value):
    root = value * lax.rsqrt(jnp.maximum(jnp.abs(value), 1e-20))
    return jnp.round(root).astype(I16)


def decode(code):
    root = code.astype(jnp.int32).astype(F32)
    return root * jnp.abs(root)


def step_of(rows, columns):
    step = 16
    while rows % (step * 2) == 0 and step * 2 * columns <= 16 * 2048:
        step *= 2
    return step


def add_into(target, others):
    step = step_of(*target.shape)

    def some(i, carry):
        rows = pl.ds(pl.multiple_of(i * step, step), step)
        total = decode(target[rows, :])
        for other in others:
            total = total + decode(other[rows, :])
        target[rows, :] = encode(total)
        return carry

    lax.fori_loop(0, target.shape[0] // step, some, 0)


def kernel(
    go_hbm, pre_hbm, codes_ref, exp_hbm, gp_ref, gw_ref, ge_ref,
    go_ref, pre_ref, exp_ref, act, pqx, pqy, g, w, gsrc, cbuf,
    x1a, x1b, xm, xp, xc, y1, ya, yb, ym, yp,
    ssem, rsem, csem, isem,
):
    j = lax.axis_index("dp")
    t = lax.axis_index("tensor")
    x, yh = j // 2, j % 2
    other = 1 - yh
    z, yl, core = t // 4, (t // 2) % 2, t % 2

    def blk(dx, hi):
        return ((x + dx) % 4) * 2 + hi

    def ten(dz):
        return ((z + dz) % 4) * 4 + yl * 2 + core

    east, west = (blk(1, yh), t), (blk(3, yh), t)
    across = (blk(0, other), t)
    up, down = (j, ten(1)), (j, ten(3))
    beside = (j, z * 4 + (1 - yl) * 2 + core)
    twin = (j, z * 4 + yl * 2 + 1 - core)
    peers = [((j + k) % 8, t) for k in range(1, 8)]

    barrier = pltpu.get_barrier_semaphore()
    for device in (*peers, up, down, beside, twin):
        pl.semaphore_signal(barrier, inc=1, device_id=device, device_id_type=MESH)

    copies = {}

    def send(name, src, dst, device):
        n = len(copies)
        copy = pltpu.make_async_remote_copy(
            src_ref=src, dst_ref=dst, send_sem=ssem.at[n], recv_sem=rsem.at[n],
            device_id=device, device_id_type=MESH,
        )
        copy.start()
        copies[name] = copy

    def same(name, view, device):
        send(name, view, view, device)

    def arrive(*names):
        for name in names:
            copies[name].wait_recv()

    spans = [pl.ds(AX, EARLY), pl.ds(AX + EARLY, AY1 - EARLY), pl.ds(0, AX), pl.ds(AX + AY1, AY2)]
    pieces = []
    for n, span in enumerate(spans):
        pieces.append(pltpu.make_async_copy(pre_hbm.at[:, span], pre_ref.at[:, span], isem.at[n]))
    rows_load = pltpu.make_async_copy(go_hbm, go_ref, isem.at[5])
    exponents_load = pltpu.make_async_copy(exp_hbm, exp_ref, isem.at[4])
    for load in (pieces[0], rows_load, *pieces[1:], exponents_load):
        load.start()

    def fetch(i):
        slot = lax.rem(i, SLOTS)
        rows = pl.ds(pl.multiple_of(i * CHUNK, CHUNK), CHUNK)
        return pltpu.make_async_copy(codes_ref.at[rows, :], cbuf.at[slot], csem.at[slot])

    for i in range(SLOTS):
        fetch(i).start()

    def transpose(i, carry):
        columns = pl.ds(pl.multiple_of(i * LANES, LANES), LANES)
        positive = jnp.maximum(pre_ref[:, columns].astype(F32), 0.0)
        act[j, columns, :] = (positive * positive).astype(BF16).T
        return carry

    def piece(first, size):
        def rows(b, part=None):
            if part is None:
                return act.at[b, pl.ds(first, size), :]
            return act.at[b, pl.ds(first + part * (size // 2), size // 2), :]

        return rows

    y1_rows, x_rows, y2_rows = piece(AX, AY1), piece(0, AX), piece(AX + AY1, AY2)

    pieces[0].wait()
    lax.fori_loop(AX // LANES, (AX + EARLY) // LANES, transpose, 0)

    def early(name, start, end):
        view = act.at[j, pl.ds(AX + start, end - start), :]
        same(name, view, across)
        same(f"{name}+", view, east)
        same(f"{name}-", view, west)

    pl.semaphore_wait(barrier, 11)
    early("ay0", 0, EARLY)

    rows_load.wait()
    total = jnp.zeros((16, 1), F32)
    for d in range(8):
        block = go_ref[:, d * WIDTH : (d + 1) * WIDTH]
        total = total + jnp.sum(jnp.abs(block.astype(F32)), axis=1, keepdims=True)
        gsrc[d, :, :WIDTH] = block
    scale = jnp.maximum(total * 0.51, 1e-36).astype(BF16)
    for d in range(8):
        gsrc[d, :, WIDTH:] = jnp.broadcast_to(scale, (16, LANES))
    mine = pl.ds(pl.multiple_of(t * 16, 16), 16)
    g[j, mine, :] = gsrc[j]


    for k in range(1, 8):
        d = (j + k) % 8
        send(f"a2a{k}", gsrc.at[d], g.at[j, mine, :], (d, t))
    pieces[1].wait()
    lax.fori_loop((AX + EARLY) // LANES, (AX + AY1) // LANES, transpose, 0)
    early("ay1", EARLY, AY1)
    pieces[2].wait()
    lax.fori_loop(0, AX // LANES, transpose, 0)
    same("ax+", x_rows(j), east)
    same("ax-", x_rows(j), west)
    pieces[3].wait()
    lax.fori_loop((AX + AY1) // LANES, FF // LANES, transpose, 0)
    exponents_load.wait()

    def dequantize(i, carry):
        fetch(i).wait()
        slot = lax.rem(i, SLOTS)
        for half in range(CHUNK // GROUP):
            exponent = exp_ref[pl.ds(i * (CHUNK // GROUP) + half, 1), :]
            power = jnp.zeros(exponent.shape, F32)
            for p in range(-7, -3):
                power = jnp.where(exponent == p, 2.0**p, power)
            code = cbuf[slot, half * GROUP : (half + 1) * GROUP, :]
            rows = pl.ds(pl.multiple_of(i * CHUNK + half * GROUP, GROUP), GROUP)
            w[rows, :] = ((code - 8).astype(F32) * power).astype(BF16)

        @pl.when(i + SLOTS < N_GW)
        def _():
            fetch(i + SLOTS).start()

        return carry

    lax.fori_loop(0, N_GW, dequantize, 0)

    def tokens(dz, hi, part=None):
        rows = pl.ds(pl.multiple_of((((z + dz) % 4) * 4 + hi * 2 + core) * 16, 16), 16)
        if part is None:
            return g.at[:, rows, :]
        return g.at[pl.ds(part * 4, 4), rows, :]

    arrive(*(f"a2a{k}" for k in range(1, 8)))
    same("gl", tokens(0, yl), beside)
    same("g+", tokens(0, yl), up)
    same("g-", tokens(0, yl), down)
    same("gc0", tokens(0, yl), twin)
    same("ay2", y2_rows(j), across)
    same("axy", x_rows(j), across)

    arrive("ay0", "ay1")
    same("ayp1+", y1_rows(blk(0, other)), east)
    same("ayp1-", y1_rows(blk(0, other)), west)
    same("ay2+", y2_rows(j), east)
    same("ay2-", y2_rows(j), west)
    arrive("g+")
    same("gf+", tokens(3, yl, 0), up)
    same("gc2", tokens(3, yl), twin)
    arrive("g-")
    same("gf-", tokens(1, yl, 1), down)
    same("gc3", tokens(1, yl), twin)
    arrive("ay0+", "ay1+")
    same("ayf1+", y1_rows(blk(3, yh), 0), east)
    arrive("ay0-", "ay1-")
    same("ayf1-", y1_rows(blk(1, yh), 1), west)

    arrive("gl")
    same("gl+", tokens(0, 1 - yl), up)
    same("gl-", tokens(0, 1 - yl), down)
    same("gc1", tokens(0, 1 - yl), twin)

    def products(dz):
        zz = (z + dz) % 4
        rows = pl.ds(pl.multiple_of(zz * 64, 64), 64)
        left = g[:, rows, pl.ds(0, WIDTH)].reshape(512, WIDTH)
        inverse = UNIT / g[:, rows, pl.ds(WIDTH, LANES)].astype(F32).reshape(512, LANES)

        def fill(target, first):
            size = target.shape[2] // 2

            def some(n, carry):
                units = pl.ds(pl.multiple_of(first + n * size, LANES), size)
                columns = pl.ds(pl.multiple_of(n * size, LANES), size)
                part = lax.dot_general(left, w[units, :], NT, preferred_element_type=F32)
                part = part * jnp.concatenate([inverse] * (size // LANES), axis=1)
                target[:, rows, columns] = encode(part).reshape(8, 64, size)
                return carry

            lax.fori_loop(0, 2, some, 0)

        fill(pqx, 0)
        fill(pqy, FX)

    arrive("gc0", "gc1")
    products(0)

    arrive("ax+")
    same("axf+", x_rows(blk(3, yh), 0), east)
    same("axy1", x_rows(blk(3, yh)), across)
    arrive("ax-")
    same("axf-", x_rows(blk(1, yh), 1), west)
    same("axy2", x_rows(blk(1, yh)), across)

    arrive("gl+")
    same("glf+", tokens(3, 1 - yl, 0), up)
    same("gc4", tokens(3, 1 - yl), twin)
    arrive("gl-")
    same("glf-", tokens(1, 1 - yl, 1), down)
    same("gc5", tokens(1, 1 - yl), twin)
    arrive("ay2")
    same("ayp2+", y2_rows(blk(0, other)), east)
    same("ayp2-", y2_rows(blk(0, other)), west)

    arrive("gc2", "gc4")
    products(3)
    arrive("gf+", "gf-", "glf+", "glf-")
    same("gc6", tokens(2, yl), twin)
    same("gc7", tokens(2, 1 - yl), twin)
    arrive("ay2+")
    same("ayf2+", y2_rows(blk(3, yh), 0), east)
    arrive("ay2-")
    same("ayf2-", y2_rows(blk(1, yh), 1), west)
    arrive("ayp1+")
    same("aypf1+", y1_rows(blk(3, other), 0), east)
    arrive("ayp1-")
    same("aypf1-", y1_rows(blk(1, other), 1), west)
    arrive("gc3", "gc5")
    products(1)
    arrive("gc6", "gc7")
    products(2)
    arrive("axf+")
    same("axy3", x_rows(blk(2, yh), 0), across)
    arrive("axf-")
    same("axy4", x_rows(blk(2, yh), 1), across)

    low, high, whole = pl.ds(0, HALF), pl.ds(HALF, HALF), pl.ds(0, ROWS)

    def first(e):
        hi = other if e else yh
        send(f"h1+{e}", pqx.at[blk(2, hi), low], x1a.at[e], east)
        send(f"h1-{e}", pqx.at[blk(2, hi), high], x1b.at[e], west)

    def second(e):
        hi = other if e else yh
        send(f"h2+{e}", pqx.at[blk(1, hi), high], xm.at[e, high, :], east)
        send(f"h2-{e}", pqx.at[blk(3, hi), low], xp.at[e, low, :], west)

    first(1)
    for k in (2, 1, 3, 0):
        send(f"s{k}", pqy.at[blk(k, other), whole], y1.at[k], across)
    arrive("ayp2+")
    same("aypf2+", y2_rows(blk(3, other), 0), east)
    arrive("ayp2-")
    same("aypf2-", y2_rows(blk(1, other), 1), west)
    first(0)
    second(1)

    def relay(e):
        hi = other if e else yh
        arrive(f"h1+{e}")
        add_into(pqx.at[blk(1, hi), low], [x1a.at[e]])
        send(f"h3+{e}", pqx.at[blk(1, hi), low], xm.at[e, low, :], east)
        arrive(f"h1-{e}")
        add_into(pqx.at[blk(3, hi), high], [x1b.at[e]])
        send(f"h3-{e}", pqx.at[blk(3, hi), high], xp.at[e, high, :], west)

    relay(1)
    arrive("s2")
    add_into(pqy.at[blk(2, yh), whole], [y1.at[2]])
    send("t1+", pqy.at[blk(2, yh), low], ya, east)
    send("t1-", pqy.at[blk(2, yh), high], yb, west)
    second(0)
    relay(0)

    def weight_tiles(first):
        def some(slot, carry):
            i = first + slot
            rows = pl.ds(pl.multiple_of(i * CHUNK, CHUNK), CHUNK)
            left = jnp.concatenate([act[b, rows, :] for b in range(8)], axis=1)
            right = g[:, :, pl.ds(0, WIDTH)].reshape(8 * ROWS, WIDTH)
            tile = jnp.dot(left, right, preferred_element_type=F32)
            gw_ref[rows, :] = tile
            product = tile * w[rows, :].astype(F32)
            ge_ref[i] = LOG_TWO * jnp.sum(product.reshape(CHUNK // GROUP, GROUP, WIDTH), axis=1)
            return carry

        lax.fori_loop(0, SLOTS, some, 0)

    arrive("axy", "axy1", "axy2", "axy3", "axy4")
    arrive(*(f"{name}{n}{way}" for name in ("ayf", "aypf") for n in "12" for way in "+-"))
    weight_tiles(0)
    weight_tiles(SLOTS)

    arrive("s1")
    add_into(pqy.at[blk(1, yh), high], [y1.at[1, high, :]])
    send("t2+", pqy.at[blk(1, yh), high], ym.at[high, :], east)

    arrive("h2+1", "h2-1", "h3+1", "h3-1")
    spans = [pl.ds(sum(PIECES[:n]), size) for n, size in enumerate(PIECES)]
    for n, part in enumerate(spans):
        add_into(pqx.at[blk(0, other), part], [xm.at[1, part], xp.at[1, part]])
        send(f"c{n}", pqx.at[blk(0, other), part], xc.at[part], across)

    arrive("s3")
    add_into(pqy.at[blk(3, yh), low], [y1.at[3, low, :]])
    send("t2-", pqy.at[blk(3, yh), low], yp.at[low, :], west)
    arrive("t1+")
    add_into(pqy.at[blk(1, yh), low], [y1.at[1, low, :], ya])
    send("t3+", pqy.at[blk(1, yh), low], ym.at[low, :], east)
    arrive("t1-")
    add_into(pqy.at[blk(3, yh), high], [y1.at[3, high, :], yb])
    send("t3-", pqy.at[blk(3, yh), high], yp.at[high, :], west)

    weight_tiles(2 * SLOTS)

    def finish(own, span, first, parts):
        size = own.shape[1]
        step = step_of(span.size, size)
        columns = pl.ds(first, size)

        def some(i, carry):
            rows = pl.ds(pl.multiple_of(span.start + i * step, 16), step)
            total = decode(own[rows, :])
            for part in parts:
                total = total + decode(part[rows, :])
            unit = g[j, rows, pl.ds(WIDTH, LANES)].astype(F32) * (2.0 / UNIT)
            positive = jnp.maximum(pre_ref[rows, columns].astype(F32), 0.0)
            unit = jnp.concatenate([unit] * (size // LANES), axis=1)
            gp_ref[rows, columns] = (total * unit * positive).astype(BF16)
            return carry

        lax.fori_loop(0, span.size // step, some, 0)

    late = {"s0", "t2+", "t2-", "t3+", "t3-", *(f"c{n}" for n in range(len(PIECES)))}
    for name in copies:
        if name not in late:
            copies[name].wait_send()
    arrive("h2+0", "h2-0", "h3+0", "h3-0")
    def finish_x(n):
        arrive(f"c{n}")
        finish(pqx.at[j], spans[n], 0, [xm.at[0], xp.at[0], xc])

    for n in range(len(PIECES) - 2):
        finish_x(n)
    arrive("s0", "t2+", "t2-", "t3+", "t3-")
    finish(pqy.at[j], whole, FX, [y1.at[0], ym, yp])
    for n in range(len(PIECES) - 2, len(PIECES)):
        finish_x(n)

    for name in copies:
        if name in late:
            copies[name].wait_send()


def place(gp, gw, ge, gp_out, gw_out, ge_out, rows, sem):
    copies = []
    for i in range(N_GW):
        part = pl.ds(i * CHUNK, CHUNK)
        copies.append(pltpu.make_async_copy(gw.at[part, :], gw_out.at[part, :], sem.at[i]))
    copies.append(pltpu.make_async_copy(gp, gp_out, sem.at[N_GW]))
    for copy in copies:
        copy.start()
    per = CHUNK // GROUP
    for i in range(N_GW):
        rows[i * per : (i + 1) * per, :] = ge[i]
    last = pltpu.make_async_copy(rows, ge_out, sem.at[N_GW + 1])
    last.start()
    for copy in (*copies, last):
        copy.wait()


def body(grad_out, pre, codes, exponents):
    vmem, hbm = pl.BlockSpec(memory_space=pltpu.VMEM), pl.BlockSpec(memory_space=pl.ANY)
    n_copies = 80
    grad_pre, grad_weight, grad_exponent = pl.pallas_call(
        kernel,
        out_shape=(
            pltpu.VMEM((ROWS, FF), BF16),
            pltpu.VMEM((FF, WIDTH), F32),
            pltpu.VMEM((N_GW, CHUNK // GROUP, WIDTH), F32),
        ),
        in_specs=[pl.BlockSpec(memory_space=pltpu.HBM)] * 4,
        out_specs=(vmem, vmem, vmem),
        scratch_shapes=[
            pltpu.VMEM((16, 8 * WIDTH), BF16),
            pltpu.VMEM((ROWS, FF), BF16),
            pltpu.VMEM(exponents.shape, jnp.int32),
            pltpu.VMEM((8, FF, ROWS), BF16),
            pltpu.VMEM((8, ROWS, FX), I16),
            pltpu.VMEM((8, ROWS, FY), I16),
            pltpu.VMEM((8, ROWS, WIDTH + LANES), BF16),
            pltpu.VMEM((FF, WIDTH), BF16),
            pltpu.VMEM((8, 16, WIDTH + LANES), BF16),
            pltpu.VMEM((SLOTS, CHUNK, WIDTH), jnp.int32),
            pltpu.VMEM((2, HALF, FX), I16),
            pltpu.VMEM((2, HALF, FX), I16),
            pltpu.VMEM((2, ROWS, FX), I16),
            pltpu.VMEM((2, ROWS, FX), I16),
            pltpu.VMEM((ROWS, FX), I16),
            pltpu.VMEM((4, ROWS, FY), I16),
            pltpu.VMEM((HALF, FY), I16),
            pltpu.VMEM((HALF, FY), I16),
            pltpu.VMEM((ROWS, FY), I16),
            pltpu.VMEM((ROWS, FY), I16),
            pltpu.SemaphoreType.DMA((n_copies,)),
            pltpu.SemaphoreType.DMA((n_copies,)),
            pltpu.SemaphoreType.DMA((SLOTS,)),
            pltpu.SemaphoreType.DMA((6,)),
        ],
        compiler_params=pltpu.CompilerParams(
            collective_id=0, has_side_effects=True, vmem_limit_bytes=46 * 2**20
        ),
        name="backward",
    )(grad_out, pre, codes, exponents)
    return pl.pallas_call(
        place,
        out_shape=(
            jax.ShapeDtypeStruct((ROWS, FF), BF16),
            jax.ShapeDtypeStruct((FF, WIDTH), F32),
            jax.ShapeDtypeStruct(exponents.shape, F32),
        ),
        in_specs=[vmem] * 3,
        out_specs=(hbm, hbm, hbm),
        scratch_shapes=[
            pltpu.VMEM(exponents.shape, F32),
            pltpu.SemaphoreType.DMA((N_GW + 2,)),
        ],
        compiler_params=pltpu.CompilerParams(vmem_limit_bytes=4 * 2**20),
        name="place",
    )(grad_pre, grad_weight, grad_exponent)


def solution(mesh):
    return jax.shard_map(
        body,
        mesh=mesh,
        in_specs=(
            P(("dp", "tensor"), None),
            P("dp", "tensor"),
            P("tensor", "dp"),
            P("tensor", "dp"),
        ),
        out_specs=(P("dp", "tensor"), P("tensor", "dp"), P("tensor", "dp")),
        check_vma=False,
    )
```

```python
import functools

import jax
import jax.numpy as jnp
from jax import lax
from jax.experimental import pallas as pl
from jax.experimental.pallas import tpu as pltpu
from jax.sharding import PartitionSpec as P

MESH = pl.DeviceIdType.MESH
LOG_TWO = 0.6931471805599453
NT = (((1,), (1,)), ((), ()))
BF16, F32, I16 = jnp.bfloat16, jnp.float32, jnp.int16

FF = 2304
WIDTH = 1152
ROWS = 256
HALF = ROWS // 2
GROUP = 128
LANES = 128
FX = 1280
FY = FF - FX
PIECES = (112, 80, 48, 16)
AX = 896
AY1 = 768
EARLY = 128
AY2 = FF - AX - AY1
TOP = 32700.0
UNIT = TOP * TOP
CHUNK = 256
N_GW = FF // CHUNK
SLOTS = 3


def encode(value):
    root = value * lax.rsqrt(jnp.maximum(jnp.abs(value), 1e-20))
    return jnp.round(root).astype(I16)


def decode(code):
    root = code.astype(jnp.int32).astype(F32)
    return root * jnp.abs(root)


def step_of(rows, columns):
    step = 16
    while rows % (step * 2) == 0 and step * 2 * columns <= 16 * 2048:
        step *= 2
    return step


def add_into(target, others):
    step = step_of(*target.shape)

    def some(i, carry):
        rows = pl.ds(pl.multiple_of(i * step, step), step)
        total = decode(target[rows, :])
        for other in others:
            total = total + decode(other[rows, :])
        target[rows, :] = encode(total)
        return carry

    lax.fori_loop(0, target.shape[0] // step, some, 0)


def kernel(
    go_hbm, pre_hbm, codes_ref, exp_hbm, gp_ref, gw_ref, ge_ref,
    go_ref, pre_ref, exp_ref, act, pqx, pqy, g, w, gsrc, cbuf,
    x1a, x1b, xm, xp, xc, y1, ya, yb, ym, yp,
    ssem, rsem, csem, isem,
):
    j = lax.axis_index("dp")
    t = lax.axis_index("tensor")
    x, yh = j // 2, j % 2
    other = 1 - yh
    z, yl, core = t // 4, (t // 2) % 2, t % 2

    def blk(dx, hi):
        return ((x + dx) % 4) * 2 + hi

    def ten(dz):
        return ((z + dz) % 4) * 4 + yl * 2 + core

    east, west = (blk(1, yh), t), (blk(3, yh), t)
    across = (blk(0, other), t)
    up, down = (j, ten(1)), (j, ten(3))
    beside = (j, z * 4 + (1 - yl) * 2 + core)
    twin = (j, z * 4 + yl * 2 + 1 - core)
    peers = [((j + k) % 8, t) for k in range(1, 8)]

    barrier = pltpu.get_barrier_semaphore()
    for device in (*peers, up, down, beside, twin):
        pl.semaphore_signal(barrier, inc=1, device_id=device, device_id_type=MESH)

    copies = {}

    def send(name, src, dst, device):
        n = len(copies)
        copy = pltpu.make_async_remote_copy(
            src_ref=src, dst_ref=dst, send_sem=ssem.at[n], recv_sem=rsem.at[n],
            device_id=device, device_id_type=MESH,
        )
        copy.start()
        copies[name] = copy

    def same(name, view, device):
        send(name, view, view, device)

    def arrive(*names):
        for name in names:
            copies[name].wait_recv()

    spans = [pl.ds(AX, EARLY), pl.ds(AX + EARLY, AY1 - EARLY), pl.ds(0, AX), pl.ds(AX + AY1, AY2)]
    pieces = []
    for n, span in enumerate(spans):
        pieces.append(pltpu.make_async_copy(pre_hbm.at[:, span], pre_ref.at[:, span], isem.at[n]))
    rows_load = pltpu.make_async_copy(go_hbm, go_ref, isem.at[5])
    exponents_load = pltpu.make_async_copy(exp_hbm, exp_ref, isem.at[4])
    for load in (pieces[0], rows_load, *pieces[1:], exponents_load):
        load.start()

    def fetch(i):
        slot = lax.rem(i, SLOTS)
        rows = pl.ds(pl.multiple_of(i * CHUNK, CHUNK), CHUNK)
        return pltpu.make_async_copy(codes_ref.at[rows, :], cbuf.at[slot], csem.at[slot])

    for i in range(SLOTS):
        fetch(i).start()

    def transpose(i, carry):
        columns = pl.ds(pl.multiple_of(i * LANES, LANES), LANES)
        positive = jnp.maximum(pre_ref[:, columns].astype(F32), 0.0)
        act[j, columns, :] = (positive * positive).astype(BF16).T
        return carry

    def piece(first, size):
        def rows(b, part=None):
            if part is None:
                return act.at[b, pl.ds(first, size), :]
            return act.at[b, pl.ds(first + part * (size // 2), size // 2), :]

        return rows

    y1_rows, x_rows, y2_rows = piece(AX, AY1), piece(0, AX), piece(AX + AY1, AY2)

    pieces[0].wait()
    lax.fori_loop(AX // LANES, (AX + EARLY) // LANES, transpose, 0)

    def early(name, start, end):
        view = act.at[j, pl.ds(AX + start, end - start), :]
        same(name, view, across)
        same(f"{name}+", view, east)
        same(f"{name}-", view, west)

    pl.semaphore_wait(barrier, 11)
    early("ay0", 0, EARLY)

    rows_load.wait()
    total = jnp.zeros((16, 1), F32)
    for d in range(8):
        block = go_ref[:, d * WIDTH : (d + 1) * WIDTH]
        total = total + jnp.sum(jnp.abs(block.astype(F32)), axis=1, keepdims=True)
        gsrc[d, :, :WIDTH] = block
    scale = jnp.maximum(total * 0.51, 1e-36).astype(BF16)
    for d in range(8):
        gsrc[d, :, WIDTH:] = jnp.broadcast_to(scale, (16, LANES))
    mine = pl.ds(pl.multiple_of(t * 16, 16), 16)
    g[j, mine, :] = gsrc[j]


    for k in range(1, 8):
        d = (j + k) % 8
        send(f"a2a{k}", gsrc.at[d], g.at[j, mine, :], (d, t))
    pieces[1].wait()
    lax.fori_loop((AX + EARLY) // LANES, (AX + AY1) // LANES, transpose, 0)
    early("ay1", EARLY, AY1)
    pieces[2].wait()
    lax.fori_loop(0, AX // LANES, transpose, 0)
    same("ax+", x_rows(j), east)
    same("ax-", x_rows(j), west)
    pieces[3].wait()
    lax.fori_loop((AX + AY1) // LANES, FF // LANES, transpose, 0)
    exponents_load.wait()

    def dequantize(i, carry):
        fetch(i).wait()
        slot = lax.rem(i, SLOTS)
        for half in range(CHUNK // GROUP):
            exponent = exp_ref[pl.ds(i * (CHUNK // GROUP) + half, 1), :]
            power = jnp.zeros(exponent.shape, F32)
            for p in range(-7, -3):
                power = jnp.where(exponent == p, 2.0**p, power)
            code = cbuf[slot, half * GROUP : (half + 1) * GROUP, :]
            rows = pl.ds(pl.multiple_of(i * CHUNK + half * GROUP, GROUP), GROUP)
            w[rows, :] = ((code - 8).astype(F32) * power).astype(BF16)

        @pl.when(i + SLOTS < N_GW)
        def _():
            fetch(i + SLOTS).start()

        return carry

    lax.fori_loop(0, N_GW, dequantize, 0)

    def tokens(dz, hi, part=None):
        rows = pl.ds(pl.multiple_of((((z + dz) % 4) * 4 + hi * 2 + core) * 16, 16), 16)
        if part is None:
            return g.at[:, rows, :]
        return g.at[pl.ds(part * 4, 4), rows, :]

    arrive(*(f"a2a{k}" for k in range(1, 8)))
    same("gl", tokens(0, yl), beside)
    same("g+", tokens(0, yl), up)
    same("g-", tokens(0, yl), down)
    same("gc0", tokens(0, yl), twin)
    same("ay2", y2_rows(j), across)
    same("axy", x_rows(j), across)

    arrive("ay0", "ay1")
    same("ayp1+", y1_rows(blk(0, other)), east)
    same("ayp1-", y1_rows(blk(0, other)), west)
    same("ay2+", y2_rows(j), east)
    same("ay2-", y2_rows(j), west)
    arrive("g+")
    same("gf+", tokens(3, yl, 0), up)
    same("gc2", tokens(3, yl), twin)
    arrive("g-")
    same("gf-", tokens(1, yl, 1), down)
    same("gc3", tokens(1, yl), twin)
    arrive("ay0+", "ay1+")
    same("ayf1+", y1_rows(blk(3, yh), 0), east)
    arrive("ay0-", "ay1-")
    same("ayf1-", y1_rows(blk(1, yh), 1), west)

    arrive("gl")
    same("gl+", tokens(0, 1 - yl), up)
    same("gl-", tokens(0, 1 - yl), down)
    same("gc1", tokens(0, 1 - yl), twin)

    def products(dz):
        zz = (z + dz) % 4
        rows = pl.ds(pl.multiple_of(zz * 64, 64), 64)
        left = g[:, rows, pl.ds(0, WIDTH)].reshape(512, WIDTH)
        inverse = UNIT / g[:, rows, pl.ds(WIDTH, LANES)].astype(F32).reshape(512, LANES)

        def fill(target, first):
            size = target.shape[2] // 2

            def some(n, carry):
                units = pl.ds(pl.multiple_of(first + n * size, LANES), size)
                columns = pl.ds(pl.multiple_of(n * size, LANES), size)
                part = lax.dot_general(left, w[units, :], NT, preferred_element_type=F32)
                part = part * jnp.concatenate([inverse] * (size // LANES), axis=1)
                target[:, rows, columns] = encode(part).reshape(8, 64, size)
                return carry

            lax.fori_loop(0, 2, some, 0)

        fill(pqx, 0)
        fill(pqy, FX)

    arrive("gc0", "gc1")
    products(0)

    arrive("ax+")
    same("axf+", x_rows(blk(3, yh), 0), east)
    same("axy1", x_rows(blk(3, yh)), across)
    arrive("ax-")
    same("axf-", x_rows(blk(1, yh), 1), west)
    same("axy2", x_rows(blk(1, yh)), across)

    arrive("gl+")
    same("glf+", tokens(3, 1 - yl, 0), up)
    same("gc4", tokens(3, 1 - yl), twin)
    arrive("gl-")
    same("glf-", tokens(1, 1 - yl, 1), down)
    same("gc5", tokens(1, 1 - yl), twin)
    arrive("ay2")
    same("ayp2+", y2_rows(blk(0, other)), east)
    same("ayp2-", y2_rows(blk(0, other)), west)

    arrive("gc2", "gc4")
    products(3)
    arrive("gf+", "gf-", "glf+", "glf-")
    same("gc6", tokens(2, yl), twin)
    same("gc7", tokens(2, 1 - yl), twin)
    arrive("ay2+")
    same("ayf2+", y2_rows(blk(3, yh), 0), east)
    arrive("ay2-")
    same("ayf2-", y2_rows(blk(1, yh), 1), west)
    arrive("ayp1+")
    same("aypf1+", y1_rows(blk(3, other), 0), east)
    arrive("ayp1-")
    same("aypf1-", y1_rows(blk(1, other), 1), west)
    arrive("gc3", "gc5")
    products(1)
    arrive("gc6", "gc7")
    products(2)
    arrive("axf+")
    same("axy3", x_rows(blk(2, yh), 0), across)
    arrive("axf-")
    same("axy4", x_rows(blk(2, yh), 1), across)

    low, high, whole = pl.ds(0, HALF), pl.ds(HALF, HALF), pl.ds(0, ROWS)

    def first(e):
        hi = other if e else yh
        send(f"h1+{e}", pqx.at[blk(2, hi), low], x1a.at[e], east)
        send(f"h1-{e}", pqx.at[blk(2, hi), high], x1b.at[e], west)

    def second(e):
        hi = other if e else yh
        send(f"h2+{e}", pqx.at[blk(1, hi), high], xm.at[e, high, :], east)
        send(f"h2-{e}", pqx.at[blk(3, hi), low], xp.at[e, low, :], west)

    first(1)
    for k in (2, 1, 3, 0):
        send(f"s{k}", pqy.at[blk(k, other), whole], y1.at[k], across)
    arrive("ayp2+")
    same("aypf2+", y2_rows(blk(3, other), 0), east)
    arrive("ayp2-")
    same("aypf2-", y2_rows(blk(1, other), 1), west)
    first(0)
    second(1)

    def relay(e):
        hi = other if e else yh
        arrive(f"h1+{e}")
        add_into(pqx.at[blk(1, hi), low], [x1a.at[e]])
        send(f"h3+{e}", pqx.at[blk(1, hi), low], xm.at[e, low, :], east)
        arrive(f"h1-{e}")
        add_into(pqx.at[blk(3, hi), high], [x1b.at[e]])
        send(f"h3-{e}", pqx.at[blk(3, hi), high], xp.at[e, high, :], west)

    relay(1)
    arrive("s2")
    add_into(pqy.at[blk(2, yh), whole], [y1.at[2]])
    send("t1+", pqy.at[blk(2, yh), low], ya, east)
    send("t1-", pqy.at[blk(2, yh), high], yb, west)
    second(0)
    relay(0)

    def weight_tiles(first):
        def some(slot, carry):
            i = first + slot
            rows = pl.ds(pl.multiple_of(i * CHUNK, CHUNK), CHUNK)
            left = jnp.concatenate([act[b, rows, :] for b in range(8)], axis=1)
            right = g[:, :, pl.ds(0, WIDTH)].reshape(8 * ROWS, WIDTH)
            tile = jnp.dot(left, right, preferred_element_type=F32)
            gw_ref[rows, :] = tile
            product = tile * w[rows, :].astype(F32)
            ge_ref[i] = LOG_TWO * jnp.sum(product.reshape(CHUNK // GROUP, GROUP, WIDTH), axis=1)
            return carry

        lax.fori_loop(0, SLOTS, some, 0)

    arrive("axy", "axy1", "axy2", "axy3", "axy4")
    arrive(*(f"{name}{n}{way}" for name in ("ayf", "aypf") for n in "12" for way in "+-"))
    weight_tiles(0)
    weight_tiles(SLOTS)

    arrive("s1")
    add_into(pqy.at[blk(1, yh), high], [y1.at[1, high, :]])
    send("t2+", pqy.at[blk(1, yh), high], ym.at[high, :], east)

    arrive("h2+1", "h2-1", "h3+1", "h3-1")
    spans = [pl.ds(sum(PIECES[:n]), size) for n, size in enumerate(PIECES)]
    for n, part in enumerate(spans):
        add_into(pqx.at[blk(0, other), part], [xm.at[1, part], xp.at[1, part]])
        send(f"c{n}", pqx.at[blk(0, other), part], xc.at[part], across)

    arrive("s3")
    add_into(pqy.at[blk(3, yh), low], [y1.at[3, low, :]])
    send("t2-", pqy.at[blk(3, yh), low], yp.at[low, :], west)
    arrive("t1+")
    add_into(pqy.at[blk(1, yh), low], [y1.at[1, low, :], ya])
    send("t3+", pqy.at[blk(1, yh), low], ym.at[low, :], east)
    arrive("t1-")
    add_into(pqy.at[blk(3, yh), high], [y1.at[3, high, :], yb])
    send("t3-", pqy.at[blk(3, yh), high], yp.at[high, :], west)

    weight_tiles(2 * SLOTS)

    def finish(own, span, first, parts):
        size = own.shape[1]
        step = step_of(span.size, size)
        columns = pl.ds(first, size)

        def some(i, carry):
            rows = pl.ds(pl.multiple_of(span.start + i * step, 16), step)
            total = decode(own[rows, :])
            for part in parts:
                total = total + decode(part[rows, :])
            unit = g[j, rows, pl.ds(WIDTH, LANES)].astype(F32) * (2.0 / UNIT)
            positive = jnp.maximum(pre_ref[rows, columns].astype(F32), 0.0)
            unit = jnp.concatenate([unit] * (size // LANES), axis=1)
            gp_ref[rows, columns] = (total * unit * positive).astype(BF16)
            return carry

        lax.fori_loop(0, span.size // step, some, 0)

    late = {"s0", "t2+", "t2-", "t3+", "t3-", *(f"c{n}" for n in range(len(PIECES)))}
    for name in copies:
        if name not in late:
            copies[name].wait_send()
    arrive("h2+0", "h2-0", "h3+0", "h3-0")
    def finish_x(n):
        arrive(f"c{n}")
        finish(pqx.at[j], spans[n], 0, [xm.at[0], xp.at[0], xc])

    for n in range(len(PIECES) - 2):
        finish_x(n)
    arrive("s0", "t2+", "t2-", "t3+", "t3-")
    finish(pqy.at[j], whole, FX, [y1.at[0], ym, yp])
    for n in range(len(PIECES) - 2, len(PIECES)):
        finish_x(n)

    for name in copies:
        if name in late:
            copies[name].wait_send()


def place(gp, gw, ge, gp_out, gw_out, ge_out, rows, sem):
    copies = []
    for i in range(N_GW):
        part = pl.ds(i * CHUNK, CHUNK)
        copies.append(pltpu.make_async_copy(gw.at[part, :], gw_out.at[part, :], sem.at[i]))
    copies.append(pltpu.make_async_copy(gp, gp_out, sem.at[N_GW]))
    for copy in copies:
        copy.start()
    per = CHUNK // GROUP
    for i in range(N_GW):
        rows[i * per : (i + 1) * per, :] = ge[i]
    last = pltpu.make_async_copy(rows, ge_out, sem.at[N_GW + 1])
    last.start()
    for copy in (*copies, last):
        copy.wait()


def body(grad_out, pre, codes, exponents):
    vmem, hbm = pl.BlockSpec(memory_space=pltpu.VMEM), pl.BlockSpec(memory_space=pl.ANY)
    n_copies = 80
    grad_pre, grad_weight, grad_exponent = pl.pallas_call(
        kernel,
        out_shape=(
            pltpu.VMEM((ROWS, FF), BF16),
            pltpu.VMEM((FF, WIDTH), F32),
            pltpu.VMEM((N_GW, CHUNK // GROUP, WIDTH), F32),
        ),
        in_specs=[pl.BlockSpec(memory_space=pltpu.HBM)] * 4,
        out_specs=(vmem, vmem, vmem),
        scratch_shapes=[
            pltpu.VMEM((16, 8 * WIDTH), BF16),
            pltpu.VMEM((ROWS, FF), BF16),
            pltpu.VMEM(exponents.shape, jnp.int32),
            pltpu.VMEM((8, FF, ROWS), BF16),
            pltpu.VMEM((8, ROWS, FX), I16),
            pltpu.VMEM((8, ROWS, FY), I16),
            pltpu.VMEM((8, ROWS, WIDTH + LANES), BF16),
            pltpu.VMEM((FF, WIDTH), BF16),
            pltpu.VMEM((8, 16, WIDTH + LANES), BF16),
            pltpu.VMEM((SLOTS, CHUNK, WIDTH), jnp.int32),
            pltpu.VMEM((2, HALF, FX), I16),
            pltpu.VMEM((2, HALF, FX), I16),
            pltpu.VMEM((2, ROWS, FX), I16),
            pltpu.VMEM((2, ROWS, FX), I16),
            pltpu.VMEM((ROWS, FX), I16),
            pltpu.VMEM((4, ROWS, FY), I16),
            pltpu.VMEM((HALF, FY), I16),
            pltpu.VMEM((HALF, FY), I16),
            pltpu.VMEM((ROWS, FY), I16),
            pltpu.VMEM((ROWS, FY), I16),
            pltpu.SemaphoreType.DMA((n_copies,)),
            pltpu.SemaphoreType.DMA((n_copies,)),
            pltpu.SemaphoreType.DMA((SLOTS,)),
            pltpu.SemaphoreType.DMA((6,)),
        ],
        compiler_params=pltpu.CompilerParams(
            collective_id=0, has_side_effects=True, vmem_limit_bytes=46 * 2**20
        ),
        name="backward",
    )(grad_out, pre, codes, exponents)
    return pl.pallas_call(
        place,
        out_shape=(
            jax.ShapeDtypeStruct((ROWS, FF), BF16),
            jax.ShapeDtypeStruct((FF, WIDTH), F32),
            jax.ShapeDtypeStruct(exponents.shape, F32),
        ),
        in_specs=[vmem] * 3,
        out_specs=(hbm, hbm, hbm),
        scratch_shapes=[
            pltpu.VMEM(exponents.shape, F32),
            pltpu.SemaphoreType.DMA((N_GW + 2,)),
        ],
        compiler_params=pltpu.CompilerParams(vmem_limit_bytes=4 * 2**20),
        name="place",
    )(grad_pre, grad_weight, grad_exponent)


def solution(mesh):
    return jax.shard_map(
        body,
        mesh=mesh,
        in_specs=(
            P(("dp", "tensor"), None),
            P("dp", "tensor"),
            P("tensor", "dp"),
            P("tensor", "dp"),
        ),
        out_specs=(P("dp", "tensor"), P("tensor", "dp"), P("tensor", "dp")),
        check_vma=False,
    )
```

```python
import functools

import jax
import jax.numpy as jnp
from jax import lax
from jax.experimental import pallas as pl
from jax.experimental.pallas import tpu as pltpu
from jax.sharding import PartitionSpec as P

MESH = pl.DeviceIdType.MESH
LOG_TWO = 0.6931471805599453
NT = (((1,), (1,)), ((), ()))
BF16, F32, I16 = jnp.bfloat16, jnp.float32, jnp.int16

FF = 2304
WIDTH = 1152
ROWS = 256
HALF = ROWS // 2
GROUP = 128
LANES = 128
FX = 1280
FY = FF - FX
PIECES = (112, 80, 48, 16)
AX = 896
AY1 = 768
EARLY = 128
AY2 = FF - AX - AY1
TOP = 32700.0
UNIT = TOP * TOP
CHUNK = 256
N_GW = FF // CHUNK
SLOTS = 3


def encode(value):
    root = value * lax.rsqrt(jnp.maximum(jnp.abs(value), 1e-20))
    return jnp.round(root).astype(I16)


def decode(code):
    root = code.astype(jnp.int32).astype(F32)
    return root * jnp.abs(root)


def step_of(rows, columns):
    step = 16
    while rows % (step * 2) == 0 and step * 2 * columns <= 16 * 2048:
        step *= 2
    return step


def add_into(target, others):
    step = step_of(*target.shape)

    def some(i, carry):
        rows = pl.ds(pl.multiple_of(i * step, step), step)
        total = decode(target[rows, :])
        for other in others:
            total = total + decode(other[rows, :])
        target[rows, :] = encode(total)
        return carry

    lax.fori_loop(0, target.shape[0] // step, some, 0)


def kernel(
    go_hbm, pre_hbm, codes_ref, exp_hbm, gp_ref, gw_ref, ge_ref,
    go_ref, pre_ref, exp_ref, act, pqx, pqy, g, w, gsrc, cbuf,
    x1a, x1b, xm, xp, xc, y1, ya, yb, ym, yp,
    ssem, rsem, csem, isem,
):
    j = lax.axis_index("dp")
    t = lax.axis_index("tensor")
    x, yh = j // 2, j % 2
    other = 1 - yh
    z, yl, core = t // 4, (t // 2) % 2, t % 2

    def blk(dx, hi):
        return ((x + dx) % 4) * 2 + hi

    def ten(dz):
        return ((z + dz) % 4) * 4 + yl * 2 + core

    east, west = (blk(1, yh), t), (blk(3, yh), t)
    across = (blk(0, other), t)
    up, down = (j, ten(1)), (j, ten(3))
    beside = (j, z * 4 + (1 - yl) * 2 + core)
    twin = (j, z * 4 + yl * 2 + 1 - core)
    peers = [((j + k) % 8, t) for k in range(1, 8)]

    copies = {}

    def send(name, src, dst, device):
        n = len(copies)
        copy = pltpu.make_async_remote_copy(
            src_ref=src, dst_ref=dst, send_sem=ssem.at[n], recv_sem=rsem.at[n],
            device_id=device, device_id_type=MESH,
        )
        copy.start()
        copies[name] = copy

    def same(name, view, device):
        send(name, view, view, device)

    def arrive(*names):
        for name in names:
            copies[name].wait_recv()

    spans = [pl.ds(AX, EARLY), pl.ds(AX + EARLY, AY1 - EARLY), pl.ds(0, AX), pl.ds(AX + AY1, AY2)]
    pieces = []
    for n, span in enumerate(spans):
        pieces.append(pltpu.make_async_copy(pre_hbm.at[:, span], pre_ref.at[:, span], isem.at[n]))
    rows_load = pltpu.make_async_copy(go_hbm, go_ref, isem.at[5])
    exponents_load = pltpu.make_async_copy(exp_hbm, exp_ref, isem.at[4])
    pieces[0].start()

    barrier = pltpu.get_barrier_semaphore()
    for device in (*peers, up, down, beside, twin):
        pl.semaphore_signal(barrier, inc=1, device_id=device, device_id_type=MESH)

    for load in (rows_load, *pieces[1:], exponents_load):
        load.start()

    def fetch(i):
        slot = lax.rem(i, SLOTS)
        rows = pl.ds(pl.multiple_of(i * CHUNK, CHUNK), CHUNK)
        return pltpu.make_async_copy(codes_ref.at[rows, :], cbuf.at[slot], csem.at[slot])

    for i in range(SLOTS):
        fetch(i).start()

    def transpose(i, carry):
        columns = pl.ds(pl.multiple_of(i * LANES, LANES), LANES)
        positive = jnp.maximum(pre_ref[:, columns].astype(F32), 0.0)
        act[j, columns, :] = (positive * positive).astype(BF16).T
        return carry

    def piece(first, size):
        def rows(b, part=None):
            if part is None:
                return act.at[b, pl.ds(first, size), :]
            return act.at[b, pl.ds(first + part * (size // 2), size // 2), :]

        return rows

    y1_rows, x_rows, y2_rows = piece(AX, AY1), piece(0, AX), piece(AX + AY1, AY2)

    pieces[0].wait()
    lax.fori_loop(AX // LANES, (AX + EARLY) // LANES, transpose, 0)

    def early(name, start, end):
        view = act.at[j, pl.ds(AX + start, end - start), :]
        same(name, view, across)
        same(f"{name}+", view, east)
        same(f"{name}-", view, west)

    pl.semaphore_wait(barrier, 11)
    early("ay0", 0, EARLY)

    rows_load.wait()
    total = jnp.zeros((16, 1), F32)
    for d in range(8):
        block = go_ref[:, d * WIDTH : (d + 1) * WIDTH]
        total = total + jnp.sum(jnp.abs(block.astype(F32)), axis=1, keepdims=True)
        gsrc[d, :, :WIDTH] = block
    scale = jnp.maximum(total * 0.51, 1e-36).astype(BF16)
    for d in range(8):
        gsrc[d, :, WIDTH:] = jnp.broadcast_to(scale, (16, LANES))
    mine = pl.ds(pl.multiple_of(t * 16, 16), 16)
    g[j, mine, :] = gsrc[j]


    for k in range(1, 8):
        d = (j + k) % 8
        send(f"a2a{k}", gsrc.at[d], g.at[j, mine, :], (d, t))
    pieces[1].wait()
    lax.fori_loop((AX + EARLY) // LANES, (AX + AY1) // LANES, transpose, 0)
    early("ay1", EARLY, AY1)
    pieces[2].wait()
    lax.fori_loop(0, AX // LANES, transpose, 0)
    same("ax+", x_rows(j), east)
    same("ax-", x_rows(j), west)
    pieces[3].wait()
    lax.fori_loop((AX + AY1) // LANES, FF // LANES, transpose, 0)
    exponents_load.wait()

    def dequantize(i, carry):
        fetch(i).wait()
        slot = lax.rem(i, SLOTS)
        for half in range(CHUNK // GROUP):
            exponent = exp_ref[pl.ds(i * (CHUNK // GROUP) + half, 1), :]
            power = jnp.zeros(exponent.shape, F32)
            for p in range(-7, -3):
                power = jnp.where(exponent == p, 2.0**p, power)
            code = cbuf[slot, half * GROUP : (half + 1) * GROUP, :]
            rows = pl.ds(pl.multiple_of(i * CHUNK + half * GROUP, GROUP), GROUP)
            w[rows, :] = ((code - 8).astype(F32) * power).astype(BF16)

        @pl.when(i + SLOTS < N_GW)
        def _():
            fetch(i + SLOTS).start()

        return carry

    lax.fori_loop(0, N_GW, dequantize, 0)

    def tokens(dz, hi, part=None):
        rows = pl.ds(pl.multiple_of((((z + dz) % 4) * 4 + hi * 2 + core) * 16, 16), 16)
        if part is None:
            return g.at[:, rows, :]
        return g.at[pl.ds(part * 4, 4), rows, :]

    arrive(*(f"a2a{k}" for k in range(1, 8)))
    same("gl", tokens(0, yl), beside)
    same("g+", tokens(0, yl), up)
    same("g-", tokens(0, yl), down)
    same("gc0", tokens(0, yl), twin)
    same("ay2", y2_rows(j), across)
    same("axy", x_rows(j), across)

    arrive("ay0", "ay1")
    same("ayp1+", y1_rows(blk(0, other)), east)
    same("ayp1-", y1_rows(blk(0, other)), west)
    same("ay2+", y2_rows(j), east)
    same("ay2-", y2_rows(j), west)
    arrive("g+")
    same("gf+", tokens(3, yl, 0), up)
    same("gc2", tokens(3, yl), twin)
    arrive("g-")
    same("gf-", tokens(1, yl, 1), down)
    same("gc3", tokens(1, yl), twin)
    arrive("ay0+", "ay1+")
    same("ayf1+", y1_rows(blk(3, yh), 0), east)
    arrive("ay0-", "ay1-")
    same("ayf1-", y1_rows(blk(1, yh), 1), west)

    arrive("gl")
    same("gl+", tokens(0, 1 - yl), up)
    same("gl-", tokens(0, 1 - yl), down)
    same("gc1", tokens(0, 1 - yl), twin)

    def products(dz):
        zz = (z + dz) % 4
        rows = pl.ds(pl.multiple_of(zz * 64, 64), 64)
        left = g[:, rows, pl.ds(0, WIDTH)].reshape(512, WIDTH)
        inverse = UNIT / g[:, rows, pl.ds(WIDTH, LANES)].astype(F32).reshape(512, LANES)

        def fill(target, first):
            size = target.shape[2] // 2

            def some(n, carry):
                units = pl.ds(pl.multiple_of(first + n * size, LANES), size)
                columns = pl.ds(pl.multiple_of(n * size, LANES), size)
                part = lax.dot_general(left, w[units, :], NT, preferred_element_type=F32)
                part = part * jnp.concatenate([inverse] * (size // LANES), axis=1)
                target[:, rows, columns] = encode(part).reshape(8, 64, size)
                return carry

            lax.fori_loop(0, 2, some, 0)

        fill(pqx, 0)
        fill(pqy, FX)

    arrive("gc0", "gc1")
    products(0)

    arrive("ax+")
    same("axf+", x_rows(blk(3, yh), 0), east)
    same("axy1", x_rows(blk(3, yh)), across)
    arrive("ax-")
    same("axf-", x_rows(blk(1, yh), 1), west)
    same("axy2", x_rows(blk(1, yh)), across)

    arrive("gl+")
    same("glf+", tokens(3, 1 - yl, 0), up)
    same("gc4", tokens(3, 1 - yl), twin)
    arrive("gl-")
    same("glf-", tokens(1, 1 - yl, 1), down)
    same("gc5", tokens(1, 1 - yl), twin)
    arrive("ay2")
    same("ayp2+", y2_rows(blk(0, other)), east)
    same("ayp2-", y2_rows(blk(0, other)), west)

    arrive("gc2", "gc4")
    products(3)
    arrive("gf+", "gf-", "glf+", "glf-")
    same("gc6", tokens(2, yl), twin)
    same("gc7", tokens(2, 1 - yl), twin)
    arrive("ay2+")
    same("ayf2+", y2_rows(blk(3, yh), 0), east)
    arrive("ay2-")
    same("ayf2-", y2_rows(blk(1, yh), 1), west)
    arrive("ayp1+")
    same("aypf1+", y1_rows(blk(3, other), 0), east)
    arrive("ayp1-")
    same("aypf1-", y1_rows(blk(1, other), 1), west)
    arrive("gc3", "gc5")
    products(1)
    arrive("gc6", "gc7")
    products(2)
    arrive("axf+")
    same("axy3", x_rows(blk(2, yh), 0), across)
    arrive("axf-")
    same("axy4", x_rows(blk(2, yh), 1), across)

    low, high, whole = pl.ds(0, HALF), pl.ds(HALF, HALF), pl.ds(0, ROWS)

    def first(e):
        hi = other if e else yh
        send(f"h1+{e}", pqx.at[blk(2, hi), low], x1a.at[e], east)
        send(f"h1-{e}", pqx.at[blk(2, hi), high], x1b.at[e], west)

    def second(e):
        hi = other if e else yh
        send(f"h2+{e}", pqx.at[blk(1, hi), high], xm.at[e, high, :], east)
        send(f"h2-{e}", pqx.at[blk(3, hi), low], xp.at[e, low, :], west)

    first(1)
    for k in (2, 1, 3, 0):
        send(f"s{k}", pqy.at[blk(k, other), whole], y1.at[k], across)
    arrive("ayp2+")
    same("aypf2+", y2_rows(blk(3, other), 0), east)
    arrive("ayp2-")
    same("aypf2-", y2_rows(blk(1, other), 1), west)
    first(0)
    second(1)

    def relay(e):
        hi = other if e else yh
        arrive(f"h1+{e}")
        add_into(pqx.at[blk(1, hi), low], [x1a.at[e]])
        send(f"h3+{e}", pqx.at[blk(1, hi), low], xm.at[e, low, :], east)
        arrive(f"h1-{e}")
        add_into(pqx.at[blk(3, hi), high], [x1b.at[e]])
        send(f"h3-{e}", pqx.at[blk(3, hi), high], xp.at[e, high, :], west)

    relay(1)
    arrive("s2")
    add_into(pqy.at[blk(2, yh), whole], [y1.at[2]])
    send("t1+", pqy.at[blk(2, yh), low], ya, east)
    send("t1-", pqy.at[blk(2, yh), high], yb, west)
    second(0)
    relay(0)

    def weight_tiles(first):
        def some(slot, carry):
            i = first + slot
            rows = pl.ds(pl.multiple_of(i * CHUNK, CHUNK), CHUNK)
            left = jnp.concatenate([act[b, rows, :] for b in range(8)], axis=1)
            right = g[:, :, pl.ds(0, WIDTH)].reshape(8 * ROWS, WIDTH)
            tile = jnp.dot(left, right, preferred_element_type=F32)
            gw_ref[rows, :] = tile
            product = tile * w[rows, :].astype(F32)
            ge_ref[i] = LOG_TWO * jnp.sum(product.reshape(CHUNK // GROUP, GROUP, WIDTH), axis=1)
            return carry

        lax.fori_loop(0, SLOTS, some, 0)

    arrive("axy", "axy1", "axy2", "axy3", "axy4")
    arrive(*(f"{name}{n}{way}" for name in ("ayf", "aypf") for n in "12" for way in "+-"))
    weight_tiles(0)
    weight_tiles(SLOTS)

    arrive("s1")
    add_into(pqy.at[blk(1, yh), high], [y1.at[1, high, :]])
    send("t2+", pqy.at[blk(1, yh), high], ym.at[high, :], east)

    arrive("h2+1", "h2-1", "h3+1", "h3-1")
    spans = [pl.ds(sum(PIECES[:n]), size) for n, size in enumerate(PIECES)]
    for n, part in enumerate(spans):
        add_into(pqx.at[blk(0, other), part], [xm.at[1, part], xp.at[1, part]])
        send(f"c{n}", pqx.at[blk(0, other), part], xc.at[part], across)

    arrive("s3")
    add_into(pqy.at[blk(3, yh), low], [y1.at[3, low, :]])
    send("t2-", pqy.at[blk(3, yh), low], yp.at[low, :], west)
    arrive("t1+")
    add_into(pqy.at[blk(1, yh), low], [y1.at[1, low, :], ya])
    send("t3+", pqy.at[blk(1, yh), low], ym.at[low, :], east)
    arrive("t1-")
    add_into(pqy.at[blk(3, yh), high], [y1.at[3, high, :], yb])
    send("t3-", pqy.at[blk(3, yh), high], yp.at[high, :], west)

    weight_tiles(2 * SLOTS)

    def finish(own, span, first, parts):
        size = own.shape[1]
        step = step_of(span.size, size)
        columns = pl.ds(first, size)

        def some(i, carry):
            rows = pl.ds(pl.multiple_of(span.start + i * step, 16), step)
            total = decode(own[rows, :])
            for part in parts:
                total = total + decode(part[rows, :])
            unit = g[j, rows, pl.ds(WIDTH, LANES)].astype(F32) * (2.0 / UNIT)
            positive = jnp.maximum(pre_ref[rows, columns].astype(F32), 0.0)
            unit = jnp.concatenate([unit] * (size // LANES), axis=1)
            gp_ref[rows, columns] = (total * unit * positive).astype(BF16)
            return carry

        lax.fori_loop(0, span.size // step, some, 0)

    late = {"s0", "t2+", "t2-", "t3+", "t3-", *(f"c{n}" for n in range(len(PIECES)))}
    for name in copies:
        if name not in late:
            copies[name].wait_send()
    arrive("h2+0", "h2-0", "h3+0", "h3-0")
    def finish_x(n):
        arrive(f"c{n}")
        finish(pqx.at[j], spans[n], 0, [xm.at[0], xp.at[0], xc])

    for n in range(len(PIECES) - 2):
        finish_x(n)
    arrive("s0", "t2+", "t2-", "t3+", "t3-")
    finish(pqy.at[j], whole, FX, [y1.at[0], ym, yp])
    for n in range(len(PIECES) - 2, len(PIECES)):
        finish_x(n)

    for name in copies:
        if name in late:
            copies[name].wait_send()


def place(gp, gw, ge, gp_out, gw_out, ge_out, rows, sem):
    copies = []
    for i in range(N_GW):
        part = pl.ds(i * CHUNK, CHUNK)
        copies.append(pltpu.make_async_copy(gw.at[part, :], gw_out.at[part, :], sem.at[i]))
    copies.append(pltpu.make_async_copy(gp, gp_out, sem.at[N_GW]))
    for copy in copies:
        copy.start()
    per = CHUNK // GROUP
    for i in range(N_GW):
        rows[i * per : (i + 1) * per, :] = ge[i]
    last = pltpu.make_async_copy(rows, ge_out, sem.at[N_GW + 1])
    last.start()
    for copy in (*copies, last):
        copy.wait()


def body(grad_out, pre, codes, exponents):
    vmem, hbm = pl.BlockSpec(memory_space=pltpu.VMEM), pl.BlockSpec(memory_space=pl.ANY)
    n_copies = 80
    grad_pre, grad_weight, grad_exponent = pl.pallas_call(
        kernel,
        out_shape=(
            pltpu.VMEM((ROWS, FF), BF16),
            pltpu.VMEM((FF, WIDTH), F32),
            pltpu.VMEM((N_GW, CHUNK // GROUP, WIDTH), F32),
        ),
        in_specs=[pl.BlockSpec(memory_space=pltpu.HBM)] * 4,
        out_specs=(vmem, vmem, vmem),
        scratch_shapes=[
            pltpu.VMEM((16, 8 * WIDTH), BF16),
            pltpu.VMEM((ROWS, FF), BF16),
            pltpu.VMEM(exponents.shape, jnp.int32),
            pltpu.VMEM((8, FF, ROWS), BF16),
            pltpu.VMEM((8, ROWS, FX), I16),
            pltpu.VMEM((8, ROWS, FY), I16),
            pltpu.VMEM((8, ROWS, WIDTH + LANES), BF16),
            pltpu.VMEM((FF, WIDTH), BF16),
            pltpu.VMEM((8, 16, WIDTH + LANES), BF16),
            pltpu.VMEM((SLOTS, CHUNK, WIDTH), jnp.int32),
            pltpu.VMEM((2, HALF, FX), I16),
            pltpu.VMEM((2, HALF, FX), I16),
            pltpu.VMEM((2, ROWS, FX), I16),
            pltpu.VMEM((2, ROWS, FX), I16),
            pltpu.VMEM((ROWS, FX), I16),
            pltpu.VMEM((4, ROWS, FY), I16),
            pltpu.VMEM((HALF, FY), I16),
            pltpu.VMEM((HALF, FY), I16),
            pltpu.VMEM((ROWS, FY), I16),
            pltpu.VMEM((ROWS, FY), I16),
            pltpu.SemaphoreType.DMA((n_copies,)),
            pltpu.SemaphoreType.DMA((n_copies,)),
            pltpu.SemaphoreType.DMA((SLOTS,)),
            pltpu.SemaphoreType.DMA((6,)),
        ],
        compiler_params=pltpu.CompilerParams(
            collective_id=0, has_side_effects=True, vmem_limit_bytes=46 * 2**20
        ),
        name="backward",
    )(grad_out, pre, codes, exponents)
    return pl.pallas_call(
        place,
        out_shape=(
            jax.ShapeDtypeStruct((ROWS, FF), BF16),
            jax.ShapeDtypeStruct((FF, WIDTH), F32),
            jax.ShapeDtypeStruct(exponents.shape, F32),
        ),
        in_specs=[vmem] * 3,
        out_specs=(hbm, hbm, hbm),
        scratch_shapes=[
            pltpu.VMEM(exponents.shape, F32),
            pltpu.SemaphoreType.DMA((N_GW + 2,)),
        ],
        compiler_params=pltpu.CompilerParams(vmem_limit_bytes=4 * 2**20),
        name="place",
    )(grad_pre, grad_weight, grad_exponent)


def solution(mesh):
    return jax.shard_map(
        body,
        mesh=mesh,
        in_specs=(
            P(("dp", "tensor"), None),
            P("dp", "tensor"),
            P("tensor", "dp"),
            P("tensor", "dp"),
        ),
        out_specs=(P("dp", "tensor"), P("tensor", "dp"), P("tensor", "dp")),
        check_vma=False,
    )
```
